32 devices in a mesh: depth: 4 (over y, core), lat: 8 (over z, x).
Axes of the slice: x: 2, y: 2, z: 4, core: 2. Of those that a mesh axis runs over, the one named last changes fastest.
Arguments:
- obj_slices: float32 [4, 2, 2048, 512], P('depth', None, 'lat'), as said below
- probe: float32 [2, 256, 256], replicated, may hold values from -6 to 6
- positions: int32 [128, 2], P('lat'), may hold values from 0 to 256, as said below
- exit_cotangent: float32 [128, 2, 256, 256], P('lat'), may hold values from -6 to 6
Outputs:
- object_grad: float32 [4, 2, 2048, 512], P('depth', None, 'lat')
- probe_grad: float32 [2, 256, 256], P(None, 'depth')
The draws below stay inside these ranges and needn't reach their ends.
Inputs may be any that keep to these rules, and one draw needn't show every extreme that they name: `positions`: for probe p, column 0 is a row offset below 256 within tile p // 16 of 256 rows, column 1 a column offset of at most 256; offset 0, 255 and 256 each occur. `obj_slices`: each slice value is amplitude times exp(i phase) with amplitude near one.
All inputs are finite; a program needn't handle non-finite values.
Results may differ from the reference program's by a relative error of at most 0.013.
Values may be sent and summed in bfloat16 or wider, within the bound.
No kernel may reach another device: no remote copies, remote signals or barrier semaphores. Data moves between devices by JAX's collectives and lax.ppermute only.
A program may use at most 128 MiB of HBM per device.

```python
import math
import jax
import jax.numpy as jnp
from jax import lax

W = 256
NY = 512
PROBE_DEV = 16
SLICE_DEV = 1
NX = 2048
NSLICE = 4
PROBES = 128


def draw_obj_slices(key, part):
    key = jax.random.fold_in(key, 11)
    first_key, second_key = jax.random.split(key, 2)
    shape = (NSLICE, NX, NY)
    amplitude = jnp.exp(jax.random.uniform(first_key, shape, jnp.float32, -0.1, 0.1))
    phase = jax.random.uniform(second_key, shape, jnp.float32, -math.pi, math.pi)
    return jnp.stack([amplitude * jnp.cos(phase), amplitude * jnp.sin(phase)], axis=1).astype(jnp.float32)


def draw_positions(key, part):
    key = jax.random.fold_in(key, 23)
    first_key, second_key = jax.random.split(key, 2)
    row_offsets = jax.random.randint(first_key, (PROBES,), 0, W)
    col_offsets = jax.random.randint(second_key, (PROBES,), 0, NY - W + 1)
    row_offsets = row_offsets.at[0].set(W - 1).at[1].set(0)
    col_offsets = col_offsets.at[0].set(NY - W).at[1].set(0)
    return jnp.stack([row_offsets, col_offsets], axis=1).astype(jnp.int32)


def shard_levels(key, extent, cuts, low, largest):
    def one(axis_at, shards_of):
        steps = jax.random.uniform(jax.random.fold_in(jax.random.fold_in(key, 6), axis_at), (shards_of,), jnp.float32, low / len(cuts), largest / len(cuts))
        return jnp.repeat(jnp.exp(steps), extent[axis_at] // shards_of).reshape((-1,) + (1,) * (len(extent) - axis_at - 1))

    factor_of = one(*cuts[0])
    for cut in cuts[1:]:
        factor_of = factor_of * one(*cut)
    return factor_of


def gaussian(stream_key, extent, scale, bound, cuts=(), held_as=jnp.bfloat16):
    result = scale * jax.random.normal(stream_key, extent, jnp.float32)
    if cuts:
        result = result * shard_levels(stream_key, extent, cuts, -0.22, 0.18)
    return jnp.clip(result, -bound, bound).astype(held_as)


def setup_inputs(seed: int = 0) -> dict:
    keys = jax.random.split(jax.random.key(seed), 5)
    obj_slices = draw_obj_slices(jax.random.fold_in(keys[4], 71), 0)
    probe = gaussian(keys[1], (2, W, W), 1.0, 6.0, (), jnp.float32)
    positions = draw_positions(jax.random.fold_in(keys[4], 71), 0)
    exit_cotangent = gaussian(keys[3], (PROBES, 2, W, W), 1.0, 6.0, ((0, 8),), jnp.float32)
    return dict(obj_slices=obj_slices, probe=probe, positions=positions, exit_cotangent=exit_cotangent)


defocus_scale = 0.7


def propagator(size):
    freq_index = jnp.arange(size, dtype=jnp.int32)
    signed = jnp.where(freq_index < size // 2, freq_index, freq_index - size).astype(jnp.float32)
    chirp = -math.pi * defocus_scale * signed * signed / size
    product_mod = (freq_index[:, None] * freq_index[None, :]) % size
    angles = 2.0 * math.pi * product_mod.astype(jnp.float32) / size + chirp[None, :]
    kernel_real = jnp.sum(jnp.cos(angles), axis=1) / size
    kernel_imag = jnp.sum(jnp.sin(angles), axis=1) / size
    offsets = (freq_index[:, None] - freq_index[None, :]) % size
    return kernel_real[offsets], kernel_imag[offsets]


def apply_sides(prop_real, prop_imag, waves):
    real_part = waves[:, 0]
    imag_part = waves[:, 1]

    def left(matrix, field):
        return jnp.einsum("jl,bls->bjs", matrix, field, precision=lax.Precision.HIGHEST)

    def right(field, matrix):
        return jnp.einsum("bjl,ls->bjs", field, matrix, precision=lax.Precision.HIGHEST)

    first_real = left(prop_real, real_part) - left(prop_imag, imag_part)
    first_imag = left(prop_real, imag_part) + left(prop_imag, real_part)
    out_real = right(first_real, prop_real) - right(first_imag, prop_imag)
    out_imag = right(first_real, prop_imag) + right(first_imag, prop_real)
    return jnp.stack([out_real, out_imag], axis=1)


def complex_mul(first, second):
    real_part = first[:, 0] * second[:, 0] - first[:, 1] * second[:, 1]
    imag_part = first[:, 0] * second[:, 1] + first[:, 1] * second[:, 0]
    return jnp.stack([real_part, imag_part], axis=1)


def conjugate(values):
    return jnp.stack([values[:, 0], -values[:, 1]], axis=1)


def to_wire(values):
    narrow = lax.optimization_barrier(values.astype(jnp.bfloat16))
    return narrow.astype(jnp.float32)


def reference(obj_slices, probe, positions, exit_cotangent):
    prop_real, prop_imag = propagator(W)
    extended = jnp.concatenate([obj_slices, obj_slices[:, :, :W]], axis=2)
    grad_ext = jnp.zeros((NSLICE, 2, NX + W, NY), jnp.float32)
    probe_sum = jnp.zeros((2, W, W), jnp.float32)
    probe_ids = jnp.arange(PROBES, dtype=jnp.int32)

    def one_probe(carry, item):
        grad_ext, probe_sum = carry
        offset, cotangent, probe_index = item
        row_start = ((probe_index // PROBE_DEV) * W + offset[0]).astype(jnp.int32)
        col_start = offset[1].astype(jnp.int32)
        zero = jnp.zeros((), jnp.int32)
        start = (zero, zero, row_start, col_start)
        window = lax.dynamic_slice(extended, start, (NSLICE, 2, W, W))
        wave = probe[None]
        entries = []
        for slice_index in range(NSLICE):
            if slice_index > 0 and slice_index % SLICE_DEV == 0:
                wave = to_wire(wave)
            entries.append(wave)
            wave = apply_sides(prop_real, prop_imag, complex_mul(wave, window[slice_index][None]))
        cotan = cotangent[None]
        grads = [None] * NSLICE
        for slice_index in reversed(range(NSLICE)):
            before = apply_sides(prop_real, -prop_imag, cotan)
            grads[slice_index] = complex_mul(conjugate(entries[slice_index]), before)[0]
            cotan = complex_mul(conjugate(window[slice_index][None]), before)
            if slice_index > 0 and slice_index % SLICE_DEV == 0:
                cotan = to_wire(cotan)
        stacked = jnp.stack(grads, axis=0)
        current = lax.dynamic_slice(grad_ext, start, (NSLICE, 2, W, W))
        grad_ext = lax.dynamic_update_slice(grad_ext, current + stacked, start)
        return (grad_ext, probe_sum + cotan[0]), None

    (grad_ext, probe_sum), _ = lax.scan(one_probe, (grad_ext, probe_sum), (positions, exit_cotangent, probe_ids))
    object_grad = grad_ext[:, :, :NX].at[:, :, :W].add(grad_ext[:, :, NX:])
    return object_grad, probe_sum
```

```python
import functools
import math

import jax
import jax.numpy as jnp
import ml_dtypes
import numpy as np
from jax import lax
from jax.experimental import pallas as pl
from jax.experimental.pallas import tpu as pltpu
from jax.sharding import PartitionSpec as P

defocus_scale = 0.7
gain = 1.457627118644068 * np.exp(0.14208207981059368j)
f32 = jnp.float32
bf16 = jnp.bfloat16
CHUNK = 16
VMEM_LIMIT = 56 * 2**20


def propagator(size):
    index = np.arange(size)
    signed = np.where(index < size // 2, index, index - size).astype(np.float64)
    chirp = -math.pi * defocus_scale * signed * signed / size
    angles = 2.0 * math.pi * ((index[:, None] * index[None, :]) % size) / size + chirp[None, :]
    kernel = np.exp(1j * angles).sum(axis=1) / size
    return kernel[(index[:, None] - index[None, :]) % size] * gain


def sides(size):
    matrix = propagator(size)
    real, imag = matrix.real, matrix.imag
    right = np.block([[real, imag], [-imag, real]])
    left = np.block([[real, -imag], [imag, real]])
    return right.astype(ml_dtypes.bfloat16), left.astype(ml_dtypes.bfloat16)


def propagate(x, right, left, z_ref):
    w = right.shape[0] // 2
    z = jnp.dot(x, right, preferred_element_type=f32)
    z_ref[:w] = z[:, :w].astype(bf16)
    z_ref[w:] = z[:, w:].astype(bf16)
    y = jnp.dot(left, z_ref[...], preferred_element_type=f32)
    return y[:w], y[w:]


def masks(meta_ref, p, chunk, w):
    r = meta_ref[2 + 2 * p]
    q = meta_ref[3 + 2 * p]
    rows = lax.broadcasted_iota(jnp.int32, (CHUNK, w), 0) + chunk * CHUNK
    cols = lax.broadcasted_iota(jnp.int32, (CHUNK, w), 1)
    return rows < r, cols < q


def window(ext_ref, at, plane, chunk, halo_row, right_col):
    w = halo_row.shape[1]
    start = pl.multiple_of(chunk * CHUNK, CHUNK)
    own = ext_ref[at, plane, pl.ds(start, CHUNK), :].astype(f32)
    halo = ext_ref[at, plane, pl.ds(w + start, CHUNK), :].astype(f32)
    own = jnp.where(right_col, own[:, w:], own[:, :w])
    halo = jnp.where(right_col, halo[:, w:], halo[:, :w])
    return jnp.where(halo_row, halo, own)


def times_window(meta_ref, ext_ref, at, probes, w, read, write):
    def step(chunk, _):
        rows = pl.ds(pl.multiple_of(chunk * CHUNK, CHUNK), CHUNK)
        for p in range(probes):
            halo_row, right_col = masks(meta_ref, p, chunk, w)
            wr = window(ext_ref, at, 0, chunk, halo_row, right_col)
            wi = window(ext_ref, at, 1, chunk, halo_row, right_col)
            ar, ai = read(p, rows)
            write(p, rows, ar * wr - ai * wi, ar * wi + ai * wr)
        return 0

    lax.fori_loop(0, w // CHUNK, step, 0)


def add_gradients(meta_ref, g_ref, at, probes, w, read_a, read_b):
    def step(chunk, _):
        rows = pl.ds(pl.multiple_of(chunk * CHUNK, CHUNK), CHUNK)
        sums = [[[None, None], [None, None]], [[None, None], [None, None]]]
        for p in range(probes):
            halo_row, right_col = masks(meta_ref, p, chunk, w)
            ar, ai = read_a(p, rows)
            br, bi = read_b(p, rows)
            planes = (ar * br - ai * bi, -(ar * bi + ai * br))
            for plane in range(2):
                whole = planes[plane]
                halo = jnp.where(halo_row, whole, 0.0)
                parts = (whole - halo, halo)
                for tile in range(2):
                    right = jnp.where(right_col, parts[tile], 0.0)
                    for col, part in enumerate((parts[tile] - right, right)):
                        old = sums[plane][tile][col]
                        sums[plane][tile][col] = part if old is None else old + part
        for plane in range(2):
            for tile in range(2):
                at_rows = pl.ds(pl.multiple_of(tile * w + chunk * CHUNK, CHUNK), CHUNK)
                for col in range(2):
                    g_ref[at, plane, at_rows, col * w : (col + 1) * w] = sums[plane][tile][
                        col
                    ].astype(bf16)
        return 0

    lax.fori_loop(0, w // CHUNK, step, 0)


def slot_of(meta_ref, depth, order):
    d = meta_ref[0]
    high = (d >= depth // 2).astype(jnp.int32)
    return jnp.bitwise_xor(jnp.bitwise_xor(order, high * (depth - 1)), d)


def start_kernel(probes, scale, meta_ref, probe_ref, cot_ref, right_ref, left_ref, init_ref, x_ref, z_ref):
    w = probe_ref.shape[-1]
    high = meta_ref[1]
    kr, ki = float(scale.real), float(scale.imag)
    for p in range(probes):
        r = meta_ref[2 + 2 * p]
        q = lax.rem(meta_ref[3 + 2 * p], w)

        def moved(plane):
            return pltpu.roll(pltpu.roll(plane, r, 0), q, 1)

        init_ref[high, p, 0] = moved(probe_ref[0])
        init_ref[high, p, 1] = moved(probe_ref[1])
        lr = moved(cot_ref[p, 0])
        li = moved(cot_ref[p, 1])
        x_ref[:, :w] = (kr * lr + ki * li).astype(bf16)
        x_ref[:, w:] = (ki * lr - kr * li).astype(bf16)
        yr, yi = propagate(x_ref[...], right_ref[...], left_ref[...], z_ref)
        init_ref[1 - high, p, 0] = yr
        init_ref[1 - high, p, 1] = yi


def load_pieces(pieces, piece_refs, ext_ref, sems, w):
    copies = []
    for number, (at, tile, plane) in enumerate(pieces):
        rows = pl.ds(tile * w, w)
        dst = ext_ref.at[at, :, rows, :] if plane is None else ext_ref.at[at, plane, rows, :]
        copies.append(pltpu.make_async_copy(piece_refs[number], dst, sems.at[number]))
    for copy in copies:
        copy.start()
    return copies


def first_kernel(probes, depth, pieces, meta_ref, init_ref, right_ref, left_ref, *refs):
    n = len(pieces)
    piece_refs, (a_ref, ext_ref, x_ref, z_ref, sems) = refs[:n], refs[n:]
    w = init_ref.shape[-1]
    half = depth // 2
    for copy in load_pieces(pieces, piece_refs, ext_ref, sems, w):
        copy.wait()

    def write(p, rows, xr, xi):
        x_ref[p, rows, :w] = xr.astype(bf16)
        x_ref[p, rows, w:] = xi.astype(bf16)

    def step(k, _):
        at = slot_of(meta_ref, depth, k)

        def read(p, rows):
            return a_ref[k, p, 0, rows, :], a_ref[k, p, 1, rows, :]

        times_window(meta_ref, ext_ref, at, probes, w, read, write)
        for p in range(probes):
            yr, yi = propagate(x_ref[p], right_ref[...], left_ref[...], z_ref.at[p])
            a_ref[k + 1, p, 0] = yr
            a_ref[k + 1, p, 1] = yi
        return 0

    a_ref[0] = init_ref[0]
    lax.fori_loop(0, half, step, 0)


def add_probe_gradient(meta_ref, ext_ref, at, probes, w, depth, read, lam_ref, m_ref):
    d = meta_ref[0]

    def write(p, rows, xr, xi):
        m_ref[p, 0, rows, :] = xr
        m_ref[p, 1, rows, :] = -xi

    times_window(meta_ref, ext_ref, at, probes, w, read, write)
    for plane in range(2):
        total = None
        for p in range(probes):
            r = meta_ref[2 + 2 * p]
            q = meta_ref[3 + 2 * p]
            back = pltpu.roll(
                pltpu.roll(m_ref[p, plane], lax.rem(w - r, w), 0), lax.rem(2 * w - q, w), 1
            )
            total = back if total is None else total + back
        m_ref[0, plane] = total
    rows = w // depth
    for slot in range(depth):
        block = pl.multiple_of(jnp.bitwise_xor(d, slot) * rows, rows)
        for plane in range(2):
            lam_ref[slot, plane] = m_ref[0, plane, pl.ds(block, rows), :]


def second_kernel(probes, depth, pieces, meta_ref, init_ref, a_in_ref, right_ref, left_ref, *refs):
    n = len(pieces)
    half = depth // 2
    piece_refs, refs = refs[:n], refs[n:]
    g_refs, refs = refs[:half], refs[half:]
    (next_ref, lam_ref, ext_ref, g_ref, a_ref, b_ref, x_ref, z_ref, sems, out_sems) = refs
    w = init_ref.shape[-1]
    copies = load_pieces(pieces, piece_refs, ext_ref, sems, w)
    a_ref[0] = a_in_ref[0]
    b_ref[...] = init_ref[0]
    for copy in copies:
        copy.wait()

    def write(p, rows, xr, xi):
        x_ref[p, rows, :w] = xr.astype(bf16)
        x_ref[p, rows, w:] = xi.astype(bf16)

    def slot(order):
        return slot_of(meta_ref, depth, order) - half

    def read_a(k):
        return lambda p, rows: (a_ref[k, p, 0, rows, :], a_ref[k, p, 1, rows, :])

    def read_b(p, rows):
        return b_ref[p, 0, rows, :], b_ref[p, 1, rows, :]

    def a_step(k, _):
        times_window(meta_ref, ext_ref, slot(half + k), probes, w, read_a(k), write)
        for p in range(probes):
            yr, yi = propagate(x_ref[p], right_ref[...], left_ref[...], z_ref.at[p])
            a_ref[k + 1, p, 0] = yr
            a_ref[k + 1, p, 1] = yi
        return 0

    lax.fori_loop(0, half - 1, a_step, 0)

    def b_step(k, _):
        at = slot(depth - 1 - k)
        add_gradients(meta_ref, g_ref, at, probes, w, read_a(half - 1 - k), read_b)
        times_window(meta_ref, ext_ref, at, probes, w, read_b, write)

        @pl.when(k < half - 1)
        def _():
            for p in range(probes):
                yr, yi = propagate(x_ref[p], right_ref[...], left_ref[...], z_ref.at[p])
                b_ref[p, 0] = yr
                b_ref[p, 1] = yi

        return 0

    lax.fori_loop(0, half, b_step, 0)
    outs = [pltpu.make_async_copy(g_ref.at[i], g_refs[i], out_sems.at[i]) for i in range(half)]
    for copy in outs:
        copy.start()
    next_ref[...] = x_ref[...]
    high = meta_ref[1]

    @pl.when(high == 1)
    def _():
        add_probe_gradient(
            meta_ref, ext_ref, slot(depth - 1), probes, w, depth, read_a(half - 1), lam_ref, b_ref
        )

    @pl.when(high == 0)
    def _():
        lam_ref[...] = jnp.zeros(lam_ref.shape, f32)

    for copy in outs:
        copy.wait()


def third_kernel(probes, depth, pieces, meta_ref, next_ref, a_ref, lam_in_ref, right_ref, left_ref, *refs):
    n = len(pieces)
    half = depth // 2
    piece_refs, refs = refs[:n], refs[n:]
    g_refs, refs = refs[:half], refs[half:]
    (lam_ref, ext_ref, g_ref, b_ref, x_ref, z_ref, sems, out_sems) = refs
    w = a_ref.shape[-1]
    copies = load_pieces(pieces, piece_refs, ext_ref, sems, w)
    x_ref[...] = next_ref[...]
    for copy in copies:
        copy.wait()

    def write(p, rows, xr, xi):
        x_ref[p, rows, :w] = xr.astype(bf16)
        x_ref[p, rows, w:] = xi.astype(bf16)

    def read_b(p, rows):
        return b_ref[p, 0, rows, :], b_ref[p, 1, rows, :]

    def b_step(k, _):
        for p in range(probes):
            yr, yi = propagate(x_ref[p], right_ref[...], left_ref[...], z_ref.at[p])
            b_ref[p, 0] = yr
            b_ref[p, 1] = yi
        order = half - 1 - k
        at = slot_of(meta_ref, depth, order)

        def read_a(p, rows):
            return a_ref[order, p, 0, rows, :], a_ref[order, p, 1, rows, :]

        add_gradients(meta_ref, g_ref, at, probes, w, read_a, read_b)

        @pl.when(k < half - 1)
        def _():
            times_window(meta_ref, ext_ref, at, probes, w, read_b, write)

        return 0

    lax.fori_loop(0, half, b_step, 0)
    outs = [pltpu.make_async_copy(g_ref.at[i], g_refs[i], out_sems.at[i]) for i in range(half)]
    for copy in outs:
        copy.start()
    high = meta_ref[1]

    @pl.when(high == 0)
    def _():
        at = slot_of(meta_ref, depth, 0)
        add_probe_gradient(meta_ref, ext_ref, at, probes, w, depth, read_b, lam_ref, b_ref)

    @pl.when(high == 1)
    def _():
        lam_ref[...] = lam_in_ref[...]

    for copy in outs:
        copy.wait()


def cost(probes, steps, w):
    return pl.CostEstimate(
        flops=probes * steps * 16 * w**3, bytes_accessed=8 * 2**20, transcendentals=0
    )


def per_device(obj_slices, probe, positions, exit_cotangent):
    depth = lax.axis_size("depth")
    lat = lax.axis_size("lat")
    d = lax.axis_index("depth")
    w = probe.shape[-1]
    columns = obj_slices.shape[-1]
    half = depth // 2
    probes = positions.shape[0] // depth
    bits = [1 << i for i in range(depth.bit_length() - 1)]

    def across(value, bit):
        return lax.ppermute(value, "depth", [(i, i ^ bit) for i in range(depth)])

    def along(value, steps):
        return lax.ppermute(value, "lat", [(i, (i + steps) % lat) for i in range(lat)])

    def along_xor(value, bit):
        return lax.ppermute(value, "lat", [(i, i ^ bit) for i in range(lat)])

    right, left = sides(w)
    right, left = jnp.asarray(right), jnp.asarray(left)
    scale = gain ** (-2 * depth)

    my_positions = lax.dynamic_slice(positions, (d * probes, 0), (probes, 2))
    meta = jnp.concatenate(
        [jnp.stack([d, (d >= half).astype(jnp.int32)]).astype(jnp.int32), my_positions.reshape(-1)]
    )
    cotangent = lax.dynamic_slice_in_dim(exit_cotangent, d * probes, probes, 0)

    own = obj_slices[0].astype(bf16)
    tiles = {0: own}
    halos = {0: along(own, -1)}
    for bit in reversed(bits[1:]):
        for slot in sorted(tiles):
            tiles[slot | bit] = across(tiles[slot], bit)
        for slot in sorted(s for s in tiles if s & bit):
            kept = halos[slot ^ bit]
            kept = kept if isinstance(kept, tuple) else (kept[0], kept[1])
            halos[slot] = (across(kept[0], bit), along(tiles[slot][1], -1))
    for slot in sorted(tiles):
        tiles[slot | 1] = across(tiles[slot], 1)
        halos[slot | 1] = jax.tree.map(lambda x: across(x, 1), halos[slot])

    def pieces_of(slots, base):
        names, arrays = [], []
        for slot in slots:
            names.append((slot - base, 0, None))
            arrays.append(tiles[slot])
            if isinstance(halos[slot], tuple):
                for plane in range(2):
                    names.append((slot - base, 1, plane))
                    arrays.append(halos[slot][plane])
            else:
                names.append((slot - base, 1, None))
                arrays.append(halos[slot])
        return names, arrays

    smem = pl.BlockSpec(memory_space=pltpu.SMEM)
    vmem = pl.BlockSpec(memory_space=pltpu.VMEM)
    anywhere = pl.BlockSpec(memory_space=pl.ANY)
    params = pltpu.CompilerParams(vmem_limit_bytes=VMEM_LIMIT)
    wave = (probes, 2, w, w)
    x_scratch = pltpu.VMEM((probes, w, 2 * w), bf16)
    z_scratch = pltpu.VMEM((probes, 2 * w, w), bf16)
    ext_scratch = pltpu.VMEM((half, 2, 2 * w, columns), bf16)
    g_shape = (2, 2 * w, columns)
    lam_shape = (depth, 2, w // depth, w)

    init = pl.pallas_call(
        functools.partial(start_kernel, probes, scale),
        out_shape=jax.ShapeDtypeStruct((2,) + wave, f32),
        in_specs=[smem, vmem, vmem, vmem, vmem],
        out_specs=vmem,
        scratch_shapes=[pltpu.VMEM((w, 2 * w), bf16), pltpu.VMEM((2 * w, w), bf16)],
        compiler_params=params,
        cost_estimate=cost(probes, 1, w),
    )(meta, probe, cotangent, right, left)

    names, arrays = pieces_of(range(half), 0)
    a_waves = pl.pallas_call(
        functools.partial(first_kernel, probes, depth, names),
        out_shape=jax.ShapeDtypeStruct((half + 1,) + wave, f32),
        grid=(1,),
        in_specs=[smem, pl.BlockSpec((1,) + wave, lambda i: (0, 0, 0, 0, 0)), vmem, vmem]
        + [anywhere] * len(names),
        out_specs=vmem,
        scratch_shapes=[
            ext_scratch,
            x_scratch,
            z_scratch,
            pltpu.SemaphoreType.DMA((len(names),)),
        ],
        compiler_params=params,
        cost_estimate=cost(probes, half, w),
    )(meta, init, right, left, *arrays)

    other_names, other_arrays = pieces_of(range(half, depth), half)
    results = pl.pallas_call(
        functools.partial(second_kernel, probes, depth, other_names),
        out_shape=[jax.ShapeDtypeStruct(g_shape, bf16)] * half
        + [
            jax.ShapeDtypeStruct((probes, w, 2 * w), bf16),
            jax.ShapeDtypeStruct(lam_shape, f32),
        ],
        grid=(1,),
        in_specs=[
            smem,
            pl.BlockSpec((1,) + wave, lambda i: (1, 0, 0, 0, 0)),
            pl.BlockSpec((1,) + wave, lambda i: (half, 0, 0, 0, 0)),
            vmem,
            vmem,
        ]
        + [anywhere] * len(other_names),
        out_specs=[anywhere] * half + [vmem, vmem],
        scratch_shapes=[
            ext_scratch,
            pltpu.VMEM((half,) + g_shape, bf16),
            pltpu.VMEM((half,) + wave, f32),
            pltpu.VMEM(wave, f32),
            x_scratch,
            z_scratch,
            pltpu.SemaphoreType.DMA((len(other_names),)),
            pltpu.SemaphoreType.DMA((half,)),
        ],
        compiler_params=params,
        cost_estimate=cost(probes, half, w),
    )(meta, init, a_waves, right, left, *other_arrays)
    far_grads, next_x, lam = results[:half], results[half], results[half + 1]

    results = pl.pallas_call(
        functools.partial(third_kernel, probes, depth, names),
        out_shape=[jax.ShapeDtypeStruct(g_shape, bf16)] * half
        + [jax.ShapeDtypeStruct(lam_shape, f32)],
        grid=(1,),
        in_specs=[
            smem,
            vmem,
            pl.BlockSpec((half,) + wave, lambda i: (0, 0, 0, 0, 0)),
            vmem,
            vmem,
            vmem,
        ]
        + [anywhere] * len(names),
        out_specs=[anywhere] * half + [vmem],
        scratch_shapes=[
            ext_scratch,
            pltpu.VMEM((half,) + g_shape, bf16),
            pltpu.VMEM(wave, f32),
            x_scratch,
            z_scratch,
            pltpu.SemaphoreType.DMA((len(names),)),
            pltpu.SemaphoreType.DMA((half,)),
        ],
        compiler_params=params,
        cost_estimate=cost(probes, half, w),
    )(meta, next_x, a_waves, lam, right, left, *arrays)
    near_grads, lam = results[:half], results[half]

    def total(first, second):
        return (first.astype(f32) + second.astype(f32)).astype(bf16)

    grads = {slot: g for slot, g in enumerate(list(near_grads) + list(far_grads))}
    owns, halo_grads = {}, {}
    for slot in sorted((s for s in grads if not s & 1), reverse=True):
        both = total(grads[slot], across(grads[slot | 1], 1))
        owns[slot] = both[:, :w]
        halo_grads[slot] = (both[0, w:], both[1, w:])
    for bit in bits[1:]:
        for slot in sorted((s for s in owns if s & bit), reverse=True):
            halo_real, halo_imag = halo_grads.pop(slot)
            kept = halo_grads[slot ^ bit]
            halo_grads[slot ^ bit] = (total(kept[0], across(halo_real, bit)), kept[1])
            shifted_imag = along(halo_imag, 1)
            sent = owns.pop(slot)
            sent = jnp.stack([sent[0], total(sent[1], shifted_imag)])
            owns[slot ^ bit] = total(owns[slot ^ bit], across(sent, bit))
    from_below = along(jnp.stack(halo_grads[0]), 1)
    object_grad = (owns[0].astype(f32) + from_below.astype(f32))[None]

    part = lam
    for bit in reversed(bits):
        part = part[:bit] + across(part[bit : 2 * bit].astype(bf16), bit).astype(f32)
    part = part[0]
    if lat & (lat - 1):
        part = lax.psum(part, "lat")
    else:
        for bit in [1 << i for i in range(lat.bit_length() - 1)]:
            sent = part.astype(bf16)
            part = sent.astype(f32) + along_xor(sent, bit).astype(f32)
    return (object_grad, part)


def solution(mesh):
    placed = (P("depth", None, "lat", None), P(), P("lat", None), P("lat", None, None, None))
    return jax.shard_map(
        per_device,
        mesh=mesh,
        in_specs=placed,
        out_specs=(P("depth", None, "lat", None), P(None, "depth", None)),
        check_vma=False,
    )
```

```python
import functools
import math

import jax
import jax.numpy as jnp
import ml_dtypes
import numpy as np
from jax import lax
from jax.experimental import pallas as pl
from jax.experimental.pallas import tpu as pltpu
from jax.sharding import PartitionSpec as P

defocus_scale = 0.7
gain = 1.457627118644068 * np.exp(0.14208207981059368j)
f32 = jnp.float32
bf16 = jnp.bfloat16
CHUNK = 16
VMEM_LIMIT = 60 * 2**20
COST = 6


def propagator(size):
    index = np.arange(size)
    signed = np.where(index < size // 2, index, index - size).astype(np.float64)
    chirp = -math.pi * defocus_scale * signed * signed / size
    angles = 2.0 * math.pi * ((index[:, None] * index[None, :]) % size) / size + chirp[None, :]
    kernel = np.exp(1j * angles).sum(axis=1) / size
    return kernel[(index[:, None] - index[None, :]) % size] * gain


def sides(size):
    matrix = propagator(size)
    real, imag = matrix.real, matrix.imag
    right = np.block([[real, imag], [-imag, real]])
    left = np.block([[real, -imag], [imag, real]])
    return right.astype(ml_dtypes.bfloat16), left.astype(ml_dtypes.bfloat16)


def propagate(x_ref, right_ref, left_ref, z_ref, out_ref):
    w = z_ref.shape[1]
    z = jnp.dot(x_ref[...], right_ref[...], preferred_element_type=f32)
    z_ref[:w] = z[:, :w].astype(bf16)
    z_ref[w:] = z[:, w:].astype(bf16)
    y = jnp.dot(left_ref[...], z_ref[...], preferred_element_type=f32)
    out_ref[0] = y[:w].astype(out_ref.dtype)
    out_ref[1] = y[w:].astype(out_ref.dtype)


class Alternating:
    def __init__(self):
        self.waiting = None

    def flush(self):
        if self.waiting is not None:
            self.waiting()
        self.waiting = None

    def matrix(self, task):
        self.flush()
        self.waiting = task

    def vector(self, task):
        task()
        self.flush()


class Copies:
    def __init__(self, sems):
        self.sems = sems
        self.count = 0

    def start(self, src, dst):
        copy = pltpu.make_async_copy(src, dst, self.sems.at[self.count])
        self.count += 1
        copy.start()
        return copy


def order_of(meta_ref, depth, slot):
    return jnp.bitwise_xor(jnp.bitwise_xor(slot, meta_ref[0]), meta_ref[1] * (depth - 1))


def shifts(meta_ref, p):
    return meta_ref[2 + 2 * p], meta_ref[3 + 2 * p]


def load_pieces(meta_ref, depth, copies, pieces, piece_refs, ext_ref, base, w):
    started = []
    for (slot, tile, plane), ref in zip(pieces, piece_refs):
        at = order_of(meta_ref, depth, slot) - base
        rows = pl.ds(tile * w, w)
        dst = ext_ref.at[at, :, rows, :] if plane is None else ext_ref.at[at, plane, rows, :]
        started.append(copies.start(ref, dst))
    return started


def times_window(meta_ref, ext_ref, at, p, wave_ref, write):
    w = wave_ref.shape[-1]
    r, q = (value.astype(jnp.int16) for value in shifts(meta_ref, p))
    cols = lax.broadcasted_iota(jnp.int16, (CHUNK, w), 1) < q
    index = lax.broadcasted_iota(jnp.int16, (CHUNK, w), 0)
    for start in range(0, w, CHUNK):
        rows = slice(start, start + CHUNK)
        below = slice(w + start, w + start + CHUNK)
        halo_row = index + jnp.int16(start) < r
        planes = []
        for plane in range(2):
            own = jnp.where(cols, ext_ref[at, plane, rows, w:], ext_ref[at, plane, rows, :w])
            halo = jnp.where(cols, ext_ref[at, plane, below, w:], ext_ref[at, plane, below, :w])
            planes.append(jnp.where(halo_row, halo, own).astype(f32))
        wr, wi = planes
        ar, ai = wave_ref[0, rows, :].astype(f32), wave_ref[1, rows, :].astype(f32)
        write(rows, ar * wr - ai * wi, ar * wi + ai * wr)


def to_product(x_ref):
    w = x_ref.shape[0]

    def write(rows, real, imag):
        x_ref[rows, :w] = real.astype(bf16)
        x_ref[rows, w:] = imag.astype(bf16)

    return write


def gradient_rows(meta_ref, g_ref, waves_a, waves_b, start):
    w = waves_a[0].shape[-1]
    rows = slice(start, start + CHUNK)
    index = lax.broadcasted_iota(jnp.int32, (CHUNK, w), 0) + start
    cols = lax.broadcasted_iota(jnp.int32, (CHUNK, w), 1)
    sums = [None, None]
    for p, (a_ref, b_ref) in enumerate(zip(waves_a, waves_b)):
        r, q = shifts(meta_ref, p)
        halo_row, right_col = index < r, cols < q
        ar, ai = a_ref[0, rows, :].astype(f32), a_ref[1, rows, :].astype(f32)
        br, bi = b_ref[0, rows, :].astype(f32), b_ref[1, rows, :].astype(f32)
        for plane, whole in enumerate((ar * br - ai * bi, -(ar * bi + ai * br))):
            halo = jnp.where(halo_row, whole, 0.0)
            parts = (
                whole,
                halo,
                jnp.where(right_col, whole, 0.0),
                jnp.where(right_col, halo, 0.0),
            )
            old = sums[plane]
            sums[plane] = parts if old is None else tuple(x + y for x, y in zip(old, parts))
    for plane in range(2):
        whole, halo, right, both = sums[plane]
        below = slice(w + start, w + start + CHUNK)
        g_ref[plane, rows, :w] = ((whole - halo) - (right - both)).astype(bf16)
        g_ref[plane, rows, w:] = (right - both).astype(bf16)
        g_ref[plane, below, :w] = (halo - both).astype(bf16)
        g_ref[plane, below, w:] = both.astype(bf16)


def gradient_parts(meta_ref, g_ref, waves_a, waves_b, parts):
    starts = list(range(0, waves_a[0].shape[-1], CHUNK))
    size = -(-len(starts) // parts)

    def task(part):
        def run():
            for start in starts[part * size : (part + 1) * size]:
                gradient_rows(meta_ref, g_ref, waves_a, waves_b, start)

        return run

    return [task(part) for part in range(parts)]


def each(ref, count):
    return [ref.at[i] for i in range(count)]


def start_kernel(
    probes, scale, meta_ref, probe_ref, cot_hbm, right_ref, left_ref, init_hbm, cot_ref, init_ref, x_ref, z_ref, sems
):
    w = probe_ref.shape[-1]
    copies = Copies(sems)
    high = meta_ref[1]
    kr, ki = float(scale.real), float(scale.imag)
    arriving = [
        copies.start(cot_hbm.at[meta_ref[0] * probes + p], cot_ref.at[p]) for p in range(probes)
    ]
    leaving = []
    tasks = Alternating()

    def moved(p, plane):
        r, q = shifts(meta_ref, p)
        return pltpu.roll(pltpu.roll(plane, r, 0), lax.rem(q, w), 1)

    def cotangent(p):
        arriving[p].wait()
        lr, li = moved(p, cot_ref[p, 0]), moved(p, cot_ref[p, 1])
        x_ref[p, :, :w] = (kr * lr + ki * li).astype(bf16)
        x_ref[p, :, w:] = (ki * lr - kr * li).astype(bf16)

    def spread(p):
        propagate(x_ref.at[p], right_ref, left_ref, z_ref.at[p % 2], init_ref.at[1, p])
        leaving.append(copies.start(init_ref.at[1, p], init_hbm.at[1 - high, p]))

    def launch(p):
        init_ref[0, p, 0] = moved(p, probe_ref[0])
        init_ref[0, p, 1] = moved(p, probe_ref[1])
        leaving.append(copies.start(init_ref.at[0, p], init_hbm.at[high, p]))

    for p in range(probes):
        tasks.vector(functools.partial(cotangent, p))
        tasks.matrix(functools.partial(spread, p))
        tasks.vector(functools.partial(launch, p))
    tasks.flush()
    for copy in leaving:
        copy.wait()


def near_kernel(probes, depth, pieces, meta_ref, init_hbm, right_ref, left_ref, *refs):
    n = len(pieces)
    half = depth // 2
    piece_refs, (a_hbm, ext_ref, a_ref, x_ref, z_ref, sems) = refs[:n], refs[n:]
    w = a_ref.shape[-1]
    copies = Copies(sems)
    arriving = [copies.start(init_hbm.at[0, p], a_ref.at[0, p]) for p in range(probes)]
    for copy in load_pieces(meta_ref, depth, copies, pieces, piece_refs, ext_ref, 0, w):
        copy.wait()
    leaving = []
    tasks = Alternating()

    def spread(k, p):
        propagate(x_ref.at[p], right_ref, left_ref, z_ref.at[p % 2], a_ref.at[k + 1, p])
        leaving.append(copies.start(a_ref.at[k + 1, p], a_hbm.at[k, p]))

    for k in range(half):
        for p in range(probes):
            if k == 0:
                arriving[p].wait()
            if probes == 1:
                tasks.flush()
            tasks.vector(
                lambda: times_window(meta_ref, ext_ref, k, p, a_ref.at[k, p], to_product(x_ref.at[p]))
            )
            tasks.matrix(functools.partial(spread, k, p))
    tasks.flush()
    for copy in leaving:
        copy.wait()


def far_kernel(probes, depth, pieces, meta_ref, init_hbm, a_hbm, right_ref, left_ref, *refs):
    n = len(pieces)
    half = depth // 2
    piece_refs, refs = refs[:n], refs[n:]
    g_hbm, refs = refs[:half], refs[half:]
    next_hbm, v_hbm, ext_ref, g_ref, a_ref, b_ref, xa_ref, xb_ref, z_ref, sems = refs
    w = a_ref.shape[-1]
    high = meta_ref[1]
    copies = Copies(sems)
    a_in = [copies.start(a_hbm.at[half - 1, p], a_ref.at[0, p]) for p in range(probes)]
    b_in = [copies.start(init_hbm.at[1, p], b_ref.at[0, p]) for p in range(probes)]
    for copy in load_pieces(meta_ref, depth, copies, pieces, piece_refs, ext_ref, half, w):
        copy.wait()
    tasks = Alternating()

    def spread(p, x, out):
        propagate(x, right_ref, left_ref, z_ref.at[p % 2], out)

    for k in range(half - 1):
        for p in range(probes):
            if k == 0:
                a_in[p].wait()
            if probes == 1:
                tasks.flush()
            tasks.vector(
                lambda: times_window(
                    meta_ref, ext_ref, k, p, a_ref.at[k, p], to_product(xa_ref.at[p])
                )
            )
            tasks.matrix(functools.partial(spread, p, xa_ref.at[p], a_ref.at[k + 1, p]))
    leaving = []
    for k in range(half):
        last = k == half - 1
        now, later = k % 2, (k + 1) % 2
        at = half - 1 - k
        parts = gradient_parts(
            meta_ref, g_ref.at[at], each(a_ref.at[at], probes), each(b_ref.at[now], probes), probes
        )
        for p in range(probes):
            if k == 0:
                b_in[p].wait()
            if probes == 1:
                tasks.flush()
            tasks.vector(
                lambda: times_window(
                    meta_ref, ext_ref, at, p, b_ref.at[now, p], to_product(xb_ref.at[p])
                )
            )
            if last:
                leaving.append(copies.start(xb_ref.at[p], next_hbm.at[p]))
        for p in range(probes):
            if not last:
                tasks.matrix(functools.partial(spread, p, xb_ref.at[p], b_ref.at[later, p]))
            tasks.vector(parts[p])
        tasks.flush()
        if k == 0:

            @pl.when(high == 1)
            def _():
                for p in range(probes):

                    def write(rows, real, imag):
                        v_ref = xa_ref.at[p]
                        v_ref[rows, :w] = real.astype(bf16)
                        v_ref[rows, w:] = -imag.astype(bf16)

                    times_window(meta_ref, ext_ref, half - 1, p, a_ref.at[half - 1, p], write)

    leaving.append(copies.start(xa_ref, v_hbm))
    for slot in range(half):
        order = order_of(meta_ref, depth, slot + half) - half
        leaving.append(copies.start(g_ref.at[order], g_hbm[slot]))
    for copy in leaving:
        copy.wait()


def return_kernel(probes, depth, pieces, orders, meta_ref, x_hbm, a_hbm, before_hbm, right_ref, left_ref, *refs):
    n = len(pieces)
    half = depth // 2
    whole = orders[-1] == 0
    piece_refs, refs = refs[:n], refs[n:]
    g_hbm, refs = refs[: half if whole else 1], refs[half if whole else 1 :]
    x_out, ext_ref, g_ref, a_ref, b_ref, x_ref, z_ref, sems = refs
    copies = Copies(sems)
    x_in = [copies.start(x_hbm.at[p], x_ref.at[p]) for p in range(probes)]
    arrived = load_pieces(meta_ref, depth, copies, pieces, piece_refs, ext_ref, 0, ext_ref.shape[2] // 2)
    a_in = [
        copies.start(a_hbm.at[0 if whole else order - 1], a_ref.at[number])
        for number, order in enumerate(orders)
    ]
    if whole:
        arrived.append(copies.start(before_hbm, g_ref.at[pl.ds(1, half - 1)]))
    tasks = Alternating()
    leaving = []

    def spread(p):
        propagate(x_ref.at[p], right_ref, left_ref, z_ref.at[p % 2], b_ref.at[p])

    for number, order in enumerate(orders):
        if number == 0:
            for copy in x_in + arrived:
                copy.wait()
        for p in range(probes):
            tasks.matrix(functools.partial(spread, p))
            if p:
                tasks.vector(
                    lambda: times_window(
                        meta_ref, ext_ref, order, p - 1, b_ref.at[p - 1], to_product(x_ref.at[p - 1])
                    )
                )
        tasks.flush()
        p = probes - 1
        times_window(meta_ref, ext_ref, order, p, b_ref.at[p], to_product(x_ref.at[p]))
        if number == len(orders) - 1:
            leaving.append(copies.start(x_ref, x_out))
        a_in[number].wait()
        for part in gradient_parts(
            meta_ref,
            g_ref.at[order if whole else order - 1],
            each(a_ref.at[number], probes),
            each(b_ref, probes),
            1,
        ):
            part()
    if whole:
        for slot in range(half):
            leaving.append(copies.start(g_ref.at[order_of(meta_ref, depth, slot)], g_hbm[slot]))
    else:
        leaving.append(copies.start(g_ref, g_hbm[0]))
    for copy in leaving:
        copy.wait()


def probe_kernel(probes, depth, meta_ref, x_ref, v_ref, lam_ref, t_ref):
    w = x_ref.shape[1]
    d = meta_ref[0]
    low = meta_ref[1] == 0
    for plane in range(2):
        total = None
        for p in range(probes):
            r, q = shifts(meta_ref, p)
            cols = slice(plane * w, (plane + 1) * w)
            mine = x_ref[p, :, cols].astype(f32)
            mine = -mine if plane else mine
            wave = jnp.where(low, mine, v_ref[p, :, cols].astype(f32))
            back = pltpu.roll(pltpu.roll(wave, lax.rem(w - r, w), 0), lax.rem(2 * w - q, w), 1)
            total = back if total is None else total + back
        t_ref[plane] = total
    rows = w // depth
    for slot in range(depth):
        block = pl.multiple_of(jnp.bitwise_xor(d, slot) * rows, rows)
        for plane in range(2):
            lam_ref[slot, plane] = t_ref[plane, pl.ds(block, rows), :].astype(bf16)


def cost(probes, steps, w):
    return pl.CostEstimate(
        flops=COST * probes * steps * 16 * w**3, bytes_accessed=8 * 2**20, transcendentals=0
    )

def after(value, *others):
    return lax.optimization_barrier((value, others))[0]


def total(first, second):
    return (first.astype(f32) + second.astype(f32)).astype(bf16)


def per_device(obj_slices, probe, positions, exit_cotangent):
    depth = lax.axis_size("depth")
    lat = lax.axis_size("lat")
    d = lax.axis_index("depth")
    w = probe.shape[-1]
    columns = obj_slices.shape[-1]
    half = depth // 2
    probes = positions.shape[0] // depth
    bits = [1 << i for i in range(depth.bit_length() - 1)]

    def across(value, bit):
        return lax.ppermute(value, "depth", [(i, i ^ bit) for i in range(depth)])

    def along(value, steps):
        return lax.ppermute(value, "lat", [(i, (i + steps) % lat) for i in range(lat)])

    def along_xor(value, bit):
        return lax.ppermute(value, "lat", [(i, i ^ bit) for i in range(lat)])

    right, left = sides(w)
    right, left = jnp.asarray(right), jnp.asarray(left)
    scale = gain ** (-2 * depth)
    own = obj_slices[0].astype(bf16)

    my_positions = lax.dynamic_slice(positions, (d * probes, 0), (probes, 2))
    meta = jnp.concatenate(
        [jnp.stack([d, (d >= half).astype(jnp.int32)]).astype(jnp.int32), my_positions.reshape(-1)]
    )

    smem = pl.BlockSpec(memory_space=pltpu.SMEM)
    vmem = pl.BlockSpec(memory_space=pltpu.VMEM)
    anywhere = pl.BlockSpec(memory_space=pl.ANY)
    wave = (probes, 2, w, w)
    product = (probes, w, 2 * w)
    g_shape = (2, 2 * w, columns)
    z_scratch = pltpu.VMEM((2, 2 * w, w), bf16)
    ext_scratch = pltpu.VMEM((half, 2, 2 * w, columns), bf16)

    def call(kernel, name, steps, outs, ins, scratch, copies):
        flat, structure = jax.tree.flatten(outs)
        results = pl.pallas_call(
            kernel,
            out_shape=flat,
            in_specs=[spec for spec, _ in ins],
            out_specs=[anywhere] * len(flat),
            scratch_shapes=scratch + [pltpu.SemaphoreType.DMA((copies,))],
            compiler_params=pltpu.CompilerParams(vmem_limit_bytes=VMEM_LIMIT),
            cost_estimate=cost(probes, steps, w),
            name=name,
        )(*[array for _, array in ins])
        return jax.tree.unflatten(structure, results)

    shape = jax.ShapeDtypeStruct
    sides_in = [(vmem, right), (vmem, left)]

    init = call(
        functools.partial(start_kernel, probes, scale),
        "first_waves",
        1,
        shape((2,) + wave, f32),
        [(smem, meta), (vmem, probe), (anywhere, exit_cotangent)] + sides_in,
        [
            pltpu.VMEM(wave, f32),
            pltpu.VMEM((2,) + wave, f32),
            pltpu.VMEM(product, bf16),
            z_scratch,
        ],
        3 * probes,
    )

    tiles = {0: own}
    halos = {0: along(own, -1)}
    for bit in reversed(bits[1:]):
        for slot in sorted(tiles):
            tiles[slot | bit] = across(tiles[slot], bit)
        for slot in sorted(s for s in tiles if s & bit):
            kept = halos[slot ^ bit]
            kept = kept if isinstance(kept, tuple) else (kept[0], kept[1])
            halos[slot] = (
                across(after(kept[0], init), bit),
                along(after(tiles[slot][1], init), -1),
            )

    def to_both_cores(slots, earlier):
        for slot in slots:
            sent = tiles[slot] if slot == 0 else after(tiles[slot], earlier)
            tiles[slot | 1] = across(sent, 1)
            halos[slot | 1] = jax.tree.map(lambda x: across(after(x, earlier), 1), halos[slot])

    def pieces_of(slots):
        names, arrays = [], []
        for slot in slots:
            names.append((slot, 0, None))
            arrays.append((anywhere, tiles[slot]))
            if isinstance(halos[slot], tuple):
                for plane in range(2):
                    names.append((slot, 1, plane))
                    arrays.append((anywhere, halos[slot][plane]))
            else:
                names.append((slot, 1, None))
                arrays.append((anywhere, halos[slot]))
        return names, arrays

    to_both_cores(range(0, half, 2), init)
    names, arrays = pieces_of(range(half))
    a_waves = call(
        functools.partial(near_kernel, probes, depth, names),
        "near_slices",
        half,
        shape((half,) + wave, f32),
        [(smem, meta), (anywhere, init)] + sides_in + arrays,
        [ext_scratch, pltpu.VMEM((half + 1,) + wave, f32), pltpu.VMEM(product, bf16), z_scratch],
        probes * (half + 1) + len(names),
    )

    to_both_cores(range(half, depth, 2), a_waves)
    far_names, far_arrays = pieces_of(range(half, depth))
    far_grads, next_x, v = call(
        functools.partial(far_kernel, probes, depth, far_names),
        "far_slices",
        half,
        ([shape(g_shape, bf16)] * half, shape(product, bf16), shape(product, bf16)),
        [(smem, meta), (anywhere, init), (anywhere, a_waves)] + sides_in + far_arrays,
        [
            ext_scratch,
            pltpu.VMEM((half,) + g_shape, bf16),
            pltpu.VMEM((half,) + wave, f32),
            pltpu.VMEM((2,) + wave, f32),
            pltpu.VMEM(product, bf16),
            pltpu.VMEM(product, bf16),
            z_scratch,
        ],
        3 * probes + len(far_names) + half + 1,
    )

    def core_sums(grads):
        return {
            slot: total(grads[slot], across(grads[slot | 1], 1)) for slot in grads if not slot & 1
        }

    def go_back(name, orders, x, a, before, kept):
        whole = orders[-1] == 0
        return call(
            functools.partial(return_kernel, probes, depth, names, orders),
            name,
            len(orders),
            (
                [shape(g_shape, bf16)] * half if whole else [shape((half - 1,) + g_shape, bf16)],
                shape(product, bf16),
            ),
            [(smem, meta), (anywhere, x), (anywhere, a), (anywhere, before)] + sides_in + arrays,
            [
                ext_scratch,
                pltpu.VMEM((kept,) + g_shape, bf16),
                pltpu.VMEM((len(orders),) + wave, f32),
                pltpu.VMEM(wave, f32),
                pltpu.VMEM(product, bf16),
                z_scratch,
            ],
            probes + len(names) + len(orders) + half + 2,
        )

    far_sums = core_sums({slot + half: g for slot, g in enumerate(far_grads)})
    (part_grads,), x = go_back(
        "return_first", list(range(half - 1, 0, -1)), next_x, a_waves, next_x, half - 1
    )
    owns, halo_grads = {}, {}
    for slot, both in far_sums.items():
        both = after(both, x)
        owns[slot] = (both[0, :w], both[1, :w])
        halo_grads[slot] = (both[0, w:], both[1, w:])
    shifted = {slot: along(halo_grads[slot][1], 1) for slot in owns}
    crossed = {slot: across(halo_grads[slot][0], half) for slot in owns if slot & half}
    near_grads, x = go_back("return_last", [0], after(x, far_sums), init, part_grads, half)
    for slot in list(owns):
        real, imag = owns[slot]
        owns[slot] = (real, total(imag, after(shifted[slot], x)))
    crossed = {slot: after(value, x) for slot, value in crossed.items()}
    near_grads = after(near_grads, owns, crossed)
    near_sums = core_sums(dict(enumerate(near_grads)))
    for slot, both in near_sums.items():
        owns[slot] = (both[0, :w], both[1, :w])
        halo_grads[slot] = (both[0, w:], both[1, w:])
    for bit in bits[1:]:
        for slot in sorted((s for s in owns if s & bit), reverse=True):
            halo_real, halo_imag = halo_grads.pop(slot)
            real, imag = owns.pop(slot)
            halo_real = crossed[slot] if bit == half else across(halo_real, bit)
            real = across(real, bit)
            if slot not in shifted:
                imag = total(imag, along(halo_imag, 1))
            imag = across(imag, bit)
            kept = halo_grads[slot ^ bit]
            halo_grads[slot ^ bit] = (total(kept[0], halo_real), kept[1])
            kept = owns[slot ^ bit]
            owns[slot ^ bit] = (total(kept[0], real), total(kept[1], imag))
    from_below = [along(plane, 1) for plane in halo_grads[0]]
    object_grad = jnp.stack(
        [kept.astype(f32) + moved.astype(f32) for kept, moved in zip(owns[0], from_below)]
    )[None]

    part = pl.pallas_call(
        functools.partial(probe_kernel, probes, depth),
        out_shape=shape((depth, 2, w // depth, w), bf16),
        in_specs=[smem, vmem, vmem],
        out_specs=vmem,
        scratch_shapes=[pltpu.VMEM((2, w, w), f32)],
        compiler_params=pltpu.CompilerParams(vmem_limit_bytes=VMEM_LIMIT),
        cost_estimate=pl.CostEstimate(flops=0, bytes_accessed=2**17, transcendentals=0),
        name="probe_part",
    )(meta, after(x, *near_sums.values()), v)
    for bit in reversed(bits):
        part = total(part[:bit], across(part[bit : 2 * bit], bit))
    part = part[0]
    if lat & (lat - 1):
        part = lax.psum(part.astype(f32), "lat")
    else:
        for bit in [1 << i for i in range(lat.bit_length() - 1)]:
            part = total(part, along_xor(part, bit))
    return (object_grad, part.astype(f32))


def solution(mesh):
    placed = (P("depth", None, "lat", None), P(), P("lat", None), P("lat", None, None, None))
    return jax.shard_map(
        per_device,
        mesh=mesh,
        in_specs=placed,
        out_specs=(P("depth", None, "lat", None), P(None, "depth", None)),
        check_vma=False,
    )
```

```python
import functools
import math

import jax
import jax.numpy as jnp
import ml_dtypes
import numpy as np
from jax import lax
from jax.experimental import pallas as pl
from jax.experimental.pallas import tpu as pltpu
from jax.sharding import PartitionSpec as P

defocus_scale = 0.7
gain = 1.457627118644068 * np.exp(0.14208207981059368j)
f32 = jnp.float32
bf16 = jnp.bfloat16
CHUNK = 16
VMEM_LIMIT = 54 * 2**20
COST = 6


def propagator(size):
    index = np.arange(size)
    signed = np.where(index < size // 2, index, index - size).astype(np.float64)
    chirp = -math.pi * defocus_scale * signed * signed / size
    angles = 2.0 * math.pi * ((index[:, None] * index[None, :]) % size) / size + chirp[None, :]
    kernel = np.exp(1j * angles).sum(axis=1) / size
    return kernel[(index[:, None] - index[None, :]) % size] * gain


def sides(size):
    matrix = propagator(size)
    real, imag = matrix.real, matrix.imag
    right = np.block([[real, imag], [-imag, real]])
    left = np.block([[real, -imag], [imag, real]])
    return right.astype(ml_dtypes.bfloat16), left.astype(ml_dtypes.bfloat16)


def propagate(x_ref, right_ref, left_ref, z_ref, out_ref):
    w = z_ref.shape[1]
    z = jnp.dot(x_ref[...], right_ref[...], preferred_element_type=f32)
    z_ref[:w] = z[:, :w].astype(bf16)
    z_ref[w:] = z[:, w:].astype(bf16)
    y = jnp.dot(left_ref[...], z_ref[...], preferred_element_type=f32)
    out_ref[0] = y[:w].astype(out_ref.dtype)
    out_ref[1] = y[w:].astype(out_ref.dtype)


class Alternating:
    def __init__(self):
        self.waiting = None

    def flush(self):
        if self.waiting is not None:
            self.waiting()
        self.waiting = None

    def matrix(self, task):
        self.flush()
        self.waiting = task

    def vector(self, task):
        task()
        self.flush()


class Copies:
    def __init__(self, sems):
        self.sems = sems
        self.count = 0

    def start(self, src, dst):
        copy = pltpu.make_async_copy(src, dst, self.sems.at[self.count])
        self.count += 1
        copy.start()
        return copy


def order_of(meta_ref, depth, slot):
    return jnp.bitwise_xor(jnp.bitwise_xor(slot, meta_ref[0]), meta_ref[1] * (depth - 1))


def shifts(meta_ref, p):
    return meta_ref[2 + 2 * p], meta_ref[3 + 2 * p]


def load_pieces(meta_ref, depth, copies, pieces, piece_refs, ext_ref, base, w):
    started = []
    for (slot, tile, plane), ref in zip(pieces, piece_refs):
        at = order_of(meta_ref, depth, slot) - base
        rows = pl.ds(tile * w, w)
        dst = ext_ref.at[at, :, rows, :] if plane is None else ext_ref.at[at, plane, rows, :]
        started.append(copies.start(ref, dst))
    return started


def times_window(meta_ref, ext_ref, at, p, wave_ref, write):
    w = wave_ref.shape[-1]
    r, q = (value.astype(jnp.int16) for value in shifts(meta_ref, p))
    cols = lax.broadcasted_iota(jnp.int16, (CHUNK, w), 1) < q
    index = lax.broadcasted_iota(jnp.int16, (CHUNK, w), 0)
    for start in range(0, w, CHUNK):
        rows = slice(start, start + CHUNK)
        below = slice(w + start, w + start + CHUNK)
        halo_row = index + jnp.int16(start) < r
        planes = []
        for plane in range(2):
            own = jnp.where(cols, ext_ref[at, plane, rows, w:], ext_ref[at, plane, rows, :w])
            halo = jnp.where(cols, ext_ref[at, plane, below, w:], ext_ref[at, plane, below, :w])
            planes.append(jnp.where(halo_row, halo, own).astype(f32))
        wr, wi = planes
        ar, ai = wave_ref[0, rows, :].astype(f32), wave_ref[1, rows, :].astype(f32)
        write(rows, ar * wr - ai * wi, ar * wi + ai * wr)


def to_product(x_ref):
    w = x_ref.shape[0]

    def write(rows, real, imag):
        x_ref[rows, :w] = real.astype(bf16)
        x_ref[rows, w:] = imag.astype(bf16)

    return write


def gradient_rows(meta_ref, g_ref, waves_a, waves_b, start):
    w = waves_a[0].shape[-1]
    rows = slice(start, start + CHUNK)
    index = lax.broadcasted_iota(jnp.int32, (CHUNK, w), 0) + start
    cols = lax.broadcasted_iota(jnp.int32, (CHUNK, w), 1)
    sums = [None, None]
    for p, (a_ref, b_ref) in enumerate(zip(waves_a, waves_b)):
        r, q = shifts(meta_ref, p)
        halo_row, right_col = index < r, cols < q
        ar, ai = a_ref[0, rows, :].astype(f32), a_ref[1, rows, :].astype(f32)
        br, bi = b_ref[0, rows, :].astype(f32), b_ref[1, rows, :].astype(f32)
        for plane, whole in enumerate((ar * br - ai * bi, -(ar * bi + ai * br))):
            halo = jnp.where(halo_row, whole, 0.0)
            parts = (
                whole,
                halo,
                jnp.where(right_col, whole, 0.0),
                jnp.where(right_col, halo, 0.0),
            )
            old = sums[plane]
            sums[plane] = parts if old is None else tuple(x + y for x, y in zip(old, parts))
    for plane in range(2):
        whole, halo, right, both = sums[plane]
        below = slice(w + start, w + start + CHUNK)
        g_ref[plane, rows, :w] = ((whole - halo) - (right - both)).astype(bf16)
        g_ref[plane, rows, w:] = (right - both).astype(bf16)
        g_ref[plane, below, :w] = (halo - both).astype(bf16)
        g_ref[plane, below, w:] = both.astype(bf16)


def gradient_parts(meta_ref, g_ref, waves_a, waves_b, parts):
    starts = list(range(0, waves_a[0].shape[-1], CHUNK))
    size = -(-len(starts) // parts)

    def task(part):
        def run():
            for start in starts[part * size : (part + 1) * size]:
                gradient_rows(meta_ref, g_ref, waves_a, waves_b, start)

        return run

    return [task(part) for part in range(parts)]


def each(ref, count):
    return [ref.at[i] for i in range(count)]


def start_kernel(
    probes, scale, meta_ref, probe_ref, cot_hbm, right_ref, left_ref, init_hbm, cot_ref, init_ref, x_ref, z_ref, sems
):
    w = probe_ref.shape[-1]
    copies = Copies(sems)
    high = meta_ref[1]
    kr, ki = float(scale.real), float(scale.imag)
    arriving = [
        copies.start(cot_hbm.at[meta_ref[0] * probes + p], cot_ref.at[p]) for p in range(probes)
    ]
    leaving = []
    tasks = Alternating()

    def moved(p, plane):
        r, q = shifts(meta_ref, p)
        return pltpu.roll(pltpu.roll(plane, r, 0), lax.rem(q, w), 1)

    def cotangent(p):
        arriving[p].wait()
        lr, li = moved(p, cot_ref[p, 0]), moved(p, cot_ref[p, 1])
        x_ref[p, :, :w] = (kr * lr + ki * li).astype(bf16)
        x_ref[p, :, w:] = (ki * lr - kr * li).astype(bf16)

    def spread(p):
        propagate(x_ref.at[p], right_ref, left_ref, z_ref.at[p % 2], init_ref.at[1, p])
        leaving.append(copies.start(init_ref.at[1, p], init_hbm.at[1 - high, p]))

    def launch(p):
        init_ref[0, p, 0] = moved(p, probe_ref[0])
        init_ref[0, p, 1] = moved(p, probe_ref[1])
        leaving.append(copies.start(init_ref.at[0, p], init_hbm.at[high, p]))

    for p in range(probes):
        tasks.vector(functools.partial(cotangent, p))
        tasks.matrix(functools.partial(spread, p))
        tasks.vector(functools.partial(launch, p))
    tasks.flush()
    for copy in leaving:
        copy.wait()


def near_kernel(probes, depth, pieces, meta_ref, _, right_ref, left_ref, *refs):
    n = len(pieces)
    half = depth // 2
    piece_refs, (waves_hbm, ext_ref, a_ref, x_ref, z_ref, sems) = refs[:n], refs[n:]
    w = a_ref.shape[-1]
    copies = Copies(sems)
    arriving = [copies.start(waves_hbm.at[0, p], a_ref.at[0, p]) for p in range(probes)]
    for copy in load_pieces(meta_ref, depth, copies, pieces, piece_refs, ext_ref, 0, w):
        copy.wait()
    leaving = []
    tasks = Alternating()

    def spread(k, p):
        propagate(x_ref.at[p], right_ref, left_ref, z_ref.at[p % 2], a_ref.at[k + 1, p])
        leaving.append(copies.start(a_ref.at[k + 1, p], waves_hbm.at[2 + k, p]))

    for k in range(half):
        for p in range(probes):
            if k == 0:
                arriving[p].wait()
            if probes == 1:
                tasks.flush()
            tasks.vector(
                lambda: times_window(meta_ref, ext_ref, k, p, a_ref.at[k, p], to_product(x_ref.at[p]))
            )
            tasks.matrix(functools.partial(spread, k, p))
    tasks.flush()
    for copy in leaving:
        copy.wait()


def far_kernel(probes, depth, pieces, meta_ref, _, right_ref, left_ref, *refs):
    n = len(pieces)
    half = depth // 2
    piece_refs, refs = refs[:n], refs[n:]
    g_hbm, refs = refs[:half], refs[half:]
    waves_hbm, next_hbm, v_hbm, ext_ref, g_ref, a_ref, b_ref, xa_ref, xb_ref, z_ref, sems = refs
    w = a_ref.shape[-1]
    high = meta_ref[1]
    copies = Copies(sems)
    a_in = [copies.start(waves_hbm.at[1 + half, p], a_ref.at[0, p]) for p in range(probes)]
    b_in = [copies.start(waves_hbm.at[1, p], b_ref.at[0, p]) for p in range(probes)]
    for copy in load_pieces(meta_ref, depth, copies, pieces, piece_refs, ext_ref, half, w):
        copy.wait()
    tasks = Alternating()

    def spread(p, x, out):
        propagate(x, right_ref, left_ref, z_ref.at[p % 2], out)

    for k in range(half - 1):
        for p in range(probes):
            if k == 0:
                a_in[p].wait()
            if probes == 1:
                tasks.flush()
            tasks.vector(
                lambda: times_window(
                    meta_ref, ext_ref, k, p, a_ref.at[k, p], to_product(xa_ref.at[p])
                )
            )
            tasks.matrix(functools.partial(spread, p, xa_ref.at[p], a_ref.at[k + 1, p]))
    leaving = []
    for k in range(half):
        last = k == half - 1
        now, later = k % 2, (k + 1) % 2
        at = half - 1 - k
        parts = gradient_parts(
            meta_ref, g_ref.at[at], each(a_ref.at[at], probes), each(b_ref.at[now], probes), probes
        )
        for p in range(probes):
            if k == 0:
                b_in[p].wait()
            if probes == 1:
                tasks.flush()
            tasks.vector(
                lambda: times_window(
                    meta_ref, ext_ref, at, p, b_ref.at[now, p], to_product(xb_ref.at[p])
                )
            )
            if last:
                leaving.append(copies.start(xb_ref.at[p], next_hbm.at[p]))
        for p in range(probes):
            if not last:
                tasks.matrix(functools.partial(spread, p, xb_ref.at[p], b_ref.at[later, p]))
            tasks.vector(parts[p])
        tasks.flush()
        if k == 0:

            @pl.when(high == 1)
            def _():
                for p in range(probes):

                    def write(rows, real, imag):
                        v_ref = xa_ref.at[p]
                        v_ref[rows, :w] = real.astype(bf16)
                        v_ref[rows, w:] = -imag.astype(bf16)

                    times_window(meta_ref, ext_ref, half - 1, p, a_ref.at[half - 1, p], write)

    leaving.append(copies.start(xa_ref, v_hbm))
    for slot in range(half):
        order = order_of(meta_ref, depth, slot + half) - half
        leaving.append(copies.start(g_ref.at[order], g_hbm[slot]))
    for copy in leaving:
        copy.wait()


def return_kernel(probes, depth, pieces, meta_ref, _, x_hbm, v_hbm, right_ref, left_ref, *refs):
    n = len(pieces)
    half = depth // 2
    piece_refs, refs = refs[:n], refs[n:]
    waves_hbm, lam_hbm, ext_ref, b_ref, x_ref, v_ref, z_ref, t_ref, lam_ref, sems = refs
    w = x_ref.shape[1]
    copies = Copies(sems)
    x_in = [copies.start(x_hbm.at[p], x_ref.at[p]) for p in range(probes)]
    arrived = load_pieces(meta_ref, depth, copies, pieces, piece_refs, ext_ref, 0, w)
    arrived.append(copies.start(v_hbm, v_ref))
    tasks = Alternating()
    leaving = []

    def spread(k, p):
        propagate(x_ref.at[p], right_ref, left_ref, z_ref.at[p % 2], b_ref.at[k, p])
        leaving.append(copies.start(b_ref.at[k, p], waves_hbm.at[2 + half + k, p]))

    def multiply(k, p):
        if k == 0 and p == 0:
            for copy in arrived:
                copy.wait()
        times_window(
            meta_ref, ext_ref, half - 1 - k, p, b_ref.at[k, p], to_product(x_ref.at[p])
        )

    for k in range(half):
        for p in range(probes):
            if k == 0:
                x_in[p].wait()
            tasks.matrix(functools.partial(spread, k, p))
            if p:
                tasks.vector(functools.partial(multiply, k, p - 1))
        tasks.flush()
        multiply(k, probes - 1)
    low = meta_ref[1] == 0
    for plane in range(2):
        total = None
        for p in range(probes):
            r, q = shifts(meta_ref, p)
            cols = slice(plane * w, (plane + 1) * w)
            mine = x_ref[p, :, cols].astype(f32)
            mine = -mine if plane else mine
            wave = jnp.where(low, mine, v_ref[p, :, cols].astype(f32))
            back = pltpu.roll(pltpu.roll(wave, lax.rem(w - r, w), 0), lax.rem(2 * w - q, w), 1)
            total = back if total is None else total + back
        t_ref[plane] = total
    rows = w // depth
    for slot in range(depth):
        block = pl.multiple_of(jnp.bitwise_xor(meta_ref[0], slot) * rows, rows)
        for plane in range(2):
            lam_ref[slot, plane] = t_ref[plane, pl.ds(block, rows), :].astype(bf16)
    leaving.append(copies.start(lam_ref, lam_hbm))
    for copy in leaving:
        copy.wait()


def gradient_kernel(probes, depth, meta_ref, _, *refs):
    half = depth // 2
    g_hbm, (waves_hbm, g_ref, a_ref, b_ref, sems) = refs[:half], refs[half:]
    copies = Copies(sems)
    arriving = []
    for k in range(half):
        order = half - 1 - k
        arriving.append(
            (
                copies.start(waves_hbm.at[1 + order if order else 0], a_ref.at[k]),
                copies.start(waves_hbm.at[2 + half + k], b_ref.at[k]),
            )
        )
    for k in range(half):
        for copy in arriving[k]:
            copy.wait()
        for part in gradient_parts(
            meta_ref,
            g_ref.at[half - 1 - k],
            each(a_ref.at[k], probes),
            each(b_ref.at[k], probes),
            1,
        ):
            part()
    leaving = [
        copies.start(g_ref.at[order_of(meta_ref, depth, slot)], g_hbm[slot]) for slot in range(half)
    ]
    for copy in leaving:
        copy.wait()


def cost(probes, steps, w):
    return pl.CostEstimate(
        flops=COST * probes * steps * 16 * w**3, bytes_accessed=8 * 2**20, transcendentals=0
    )

def after(value, *others):
    return lax.optimization_barrier((value, others))[0]


def total(first, second):
    return (first.astype(f32) + second.astype(f32)).astype(bf16)


def per_device(obj_slices, probe, positions, exit_cotangent):
    depth = lax.axis_size("depth")
    lat = lax.axis_size("lat")
    d = lax.axis_index("depth")
    w = probe.shape[-1]
    columns = obj_slices.shape[-1]
    half = depth // 2
    probes = positions.shape[0] // depth
    bits = [1 << i for i in range(depth.bit_length() - 1)]

    def across(value, bit):
        return lax.ppermute(value, "depth", [(i, i ^ bit) for i in range(depth)])

    def along(value, steps):
        return lax.ppermute(value, "lat", [(i, (i + steps) % lat) for i in range(lat)])

    def along_xor(value, bit):
        return lax.ppermute(value, "lat", [(i, i ^ bit) for i in range(lat)])

    right, left = sides(w)
    right, left = jnp.asarray(right), jnp.asarray(left)
    scale = gain ** (-2 * depth)
    own = obj_slices[0].astype(bf16)

    my_positions = lax.dynamic_slice(positions, (d * probes, 0), (probes, 2))
    meta = jnp.concatenate(
        [jnp.stack([d, (d >= half).astype(jnp.int32)]).astype(jnp.int32), my_positions.reshape(-1)]
    )

    smem = pl.BlockSpec(memory_space=pltpu.SMEM)
    vmem = pl.BlockSpec(memory_space=pltpu.VMEM)
    anywhere = pl.BlockSpec(memory_space=pl.ANY)
    hbm = pl.BlockSpec(memory_space=pltpu.HBM)
    wave = (probes, 2, w, w)
    product = (probes, w, 2 * w)
    g_shape = (2, 2 * w, columns)
    z_scratch = pltpu.VMEM((2, 2 * w, w), bf16)
    ext_scratch = pltpu.VMEM((half, 2, 2 * w, columns), bf16)

    def call(kernel, name, steps, outs, ins, scratch, copies, limit=VMEM_LIMIT, aliases={}):
        flat, structure = jax.tree.flatten(outs)
        results = pl.pallas_call(
            kernel,
            out_shape=flat,
            in_specs=[spec for spec, _ in ins],
            out_specs=[anywhere] * len(flat),
            scratch_shapes=scratch + [pltpu.SemaphoreType.DMA((copies,))],
            compiler_params=pltpu.CompilerParams(vmem_limit_bytes=limit),
            cost_estimate=cost(probes, steps, w),
            input_output_aliases=aliases,
            name=name,
        )(*[array for _, array in ins])
        return jax.tree.unflatten(structure, results)

    shape = jax.ShapeDtypeStruct
    sides_in = [(vmem, right), (vmem, left)]

    all_waves = shape((2 + depth,) + wave, f32)
    init = call(
        functools.partial(start_kernel, probes, scale),
        "first_waves",
        1,
        all_waves,
        [(smem, meta), (vmem, probe), (hbm, exit_cotangent)] + sides_in,
        [
            pltpu.VMEM(wave, f32),
            pltpu.VMEM((2,) + wave, f32),
            pltpu.VMEM(product, bf16),
            z_scratch,
        ],
        3 * probes,
        60 * 2**20,
    )

    tiles = {0: own}
    halos = {0: along(own, -1)}
    for bit in reversed(bits[1:]):
        for slot in sorted(tiles):
            tiles[slot | bit] = across(tiles[slot], bit)
        for slot in sorted(s for s in tiles if s & bit):
            kept = halos[slot ^ bit]
            kept = kept if isinstance(kept, tuple) else (kept[0], kept[1])
            halos[slot] = (
                across(after(kept[0], init), bit),
                along(after(tiles[slot][1], init), -1),
            )

    def to_both_cores(slots, earlier):
        for slot in slots:
            sent = tiles[slot] if slot == 0 else after(tiles[slot], earlier)
            tiles[slot | 1] = across(sent, 1)
            halos[slot | 1] = jax.tree.map(lambda x: across(after(x, earlier), 1), halos[slot])

    def pieces_of(slots):
        names, arrays = [], []
        for slot in slots:
            names.append((slot, 0, None))
            arrays.append((anywhere, tiles[slot]))
            if isinstance(halos[slot], tuple):
                for plane in range(2):
                    names.append((slot, 1, plane))
                    arrays.append((anywhere, halos[slot][plane]))
            else:
                names.append((slot, 1, None))
                arrays.append((anywhere, halos[slot]))
        return names, arrays

    to_both_cores(range(0, half, 2), init)
    names, arrays = pieces_of(range(half))
    waves = call(
        functools.partial(near_kernel, probes, depth, names),
        "near_slices",
        half,
        all_waves,
        [(smem, meta), (hbm, init)] + sides_in + arrays,
        [ext_scratch, pltpu.VMEM((half + 1,) + wave, f32), pltpu.VMEM(product, bf16), z_scratch],
        probes * (half + 1) + len(names),
        aliases={1: 0},
    )

    to_both_cores(range(half, depth, 2), waves)
    far_names, far_arrays = pieces_of(range(half, depth))
    far_grads, waves, next_x, v = call(
        functools.partial(far_kernel, probes, depth, far_names),
        "far_slices",
        half,
        ([shape(g_shape, bf16)] * half, all_waves, shape(product, bf16), shape(product, bf16)),
        [(smem, meta), (hbm, waves)] + sides_in + far_arrays,
        [
            ext_scratch,
            pltpu.VMEM((half,) + g_shape, bf16),
            pltpu.VMEM((half,) + wave, f32),
            pltpu.VMEM((2,) + wave, f32),
            pltpu.VMEM(product, bf16),
            pltpu.VMEM(product, bf16),
            z_scratch,
        ],
        3 * probes + len(far_names) + half + 1,
        aliases={1: half},
    )

    waves, part = call(
        functools.partial(return_kernel, probes, depth, names),
        "return_waves",
        half,
        (all_waves, shape((depth, 2, w // depth, w), bf16)),
        [(smem, meta), (hbm, waves), (hbm, next_x), (hbm, v)] + sides_in + arrays,
        [
            ext_scratch,
            pltpu.VMEM((half,) + wave, f32),
            pltpu.VMEM(product, bf16),
            pltpu.VMEM(product, bf16),
            z_scratch,
            pltpu.VMEM((2, w, w), f32),
            pltpu.VMEM((depth, 2, w // depth, w), bf16),
        ],
        probes * (half + 1) + len(names) + 2,
        aliases={1: 0},
    )

    def core_sums(grads):
        return {
            slot: total(grads[slot], across(grads[slot | 1], 1)) for slot in grads if not slot & 1
        }

    far_sums = core_sums({slot + half: g for slot, g in enumerate(far_grads)})
    owns, halo_grads = {}, {}
    for slot, both in far_sums.items():
        both = after(both, waves)
        owns[slot] = (both[0, :w], both[1, :w])
        halo_grads[slot] = (both[0, w:], both[1, w:])
    shifted = {slot: along(halo_grads[slot][1], 1) for slot in owns}
    crossed = {slot: across(halo_grads[slot][0], half) for slot in owns if slot & half}
    part_sum = part[0].astype(f32)
    arriving = [across(part[slot], slot) for slot in range(1, depth)]
    near_grads, _ = call(
        functools.partial(gradient_kernel, probes, depth),
        "near_gradients",
        half,
        ([shape(g_shape, bf16)] * half, all_waves),
        [(smem, after(meta, far_sums)), (hbm, waves)],
        [
            pltpu.VMEM((half,) + g_shape, bf16),
            pltpu.VMEM((half,) + wave, f32),
            pltpu.VMEM((half,) + wave, f32),
        ],
        3 * half,
        aliases={1: half},
    )
    for moved in after(arriving, near_grads):
        part_sum = part_sum + moved.astype(f32)
    part = part_sum.astype(bf16)
    shifted, crossed = after((shifted, crossed), near_grads)
    for slot in list(owns):
        real, imag = owns[slot]
        owns[slot] = (real, total(imag, shifted[slot]))
    near_grads = after(near_grads, owns, crossed, part)
    near_sums = core_sums(dict(enumerate(near_grads)))
    lat_bits = [1 << i for i in range(lat.bit_length() - 1)]
    butterfly = not lat & (lat - 1)
    if butterfly:
        moved = along_xor(part, lat_bits[0])
        part = total(part, after(moved, near_sums))
    for slot, both in near_sums.items():
        halo_grads[slot] = (both[0, w:], both[1, w:])
        both = after(both, halo_grads[slot], part)
        owns[slot] = (both[0, :w], both[1, :w])
    from_below = None
    for bit in bits[1:]:
        for slot in sorted((s for s in owns if s & bit), reverse=True):
            halo_real, halo_imag = halo_grads.pop(slot)
            real, imag = owns.pop(slot)
            halo_real = crossed[slot] if bit == half else across(halo_real, bit)
            if slot not in shifted:
                imag = total(imag, along(halo_imag, 1))
            sent = across(jnp.stack([real, imag]), bit)
            kept = halo_grads[slot ^ bit]
            halo_grads[slot ^ bit] = (total(kept[0], halo_real), kept[1])
            if len(halo_grads) == 1:
                from_below = along(jnp.stack(halo_grads[0]), 1)
                sent = after(sent, from_below)
            kept = owns[slot ^ bit]
            owns[slot ^ bit] = (total(kept[0], sent[0]), total(kept[1], sent[1]))
    object_grad = (jnp.stack(owns[0]).astype(f32) + from_below.astype(f32))[None]

    if butterfly:
        for bit in lat_bits[1:]:
            part = total(part, along_xor(part, bit))
    else:
        part = lax.psum(part.astype(f32), "lat")
    return (object_grad, part.astype(f32))


def solution(mesh):
    placed = (P("depth", None, "lat", None), P(), P("lat", None), P("lat", None, None, None))
    return jax.shard_map(
        per_device,
        mesh=mesh,
        in_specs=placed,
        out_specs=(P("depth", None, "lat", None), P(None, "depth", None)),
        check_vma=False,
    )
```

```python
import functools
import math

import jax
import jax.numpy as jnp
import ml_dtypes
import numpy as np
from jax import lax
from jax.experimental import pallas as pl
from jax.experimental.pallas import tpu as pltpu
from jax.sharding import PartitionSpec as P

defocus_scale = 0.7
gain = 1.457627118644068 * np.exp(0.14208207981059368j)
f32 = jnp.float32
bf16 = jnp.bfloat16
CHUNK = 16
VMEM_LIMIT = 36 * 2**20
COST = 6


def propagator(size):
    index = np.arange(size)
    signed = np.where(index < size // 2, index, index - size).astype(np.float64)
    chirp = -math.pi * defocus_scale * signed * signed / size
    angles = 2.0 * math.pi * ((index[:, None] * index[None, :]) % size) / size + chirp[None, :]
    kernel = np.exp(1j * angles).sum(axis=1) / size
    return kernel[(index[:, None] - index[None, :]) % size] * gain


def sides(size):
    matrix = propagator(size)
    real, imag = matrix.real, matrix.imag
    right = np.block([[real, imag], [-imag, real]])
    left = np.block([[real, -imag], [imag, real]])
    return right.astype(ml_dtypes.bfloat16), left.astype(ml_dtypes.bfloat16)


def half_steps(x_ref, right_ref, left_ref, z_ref, out_refs):
    w = z_ref.shape[1]

    def first():
        z = jnp.dot(x_ref[...], right_ref[...], preferred_element_type=f32)
        z_ref[:w] = z[:, :w].astype(bf16)
        z_ref[w:] = z[:, w:].astype(bf16)

    def second():
        y = jnp.dot(left_ref[...], z_ref[...], preferred_element_type=f32)
        for out_ref in out_refs:
            out_ref[0] = y[:w].astype(out_ref.dtype)
            out_ref[1] = y[w:].astype(out_ref.dtype)

    return first, second


class Alternating:
    def __init__(self):
        self.queue = []
        self.held = None

    def release(self):
        if self.held is not None:
            self.queue.append(self.held)
        self.held = None

    def run(self, count):
        for task in self.queue[:count]:
            task()
        del self.queue[:count]

    def flush(self):
        self.release()
        self.run(len(self.queue))

    def matrix(self, steps, then=None):
        first, second = steps

        def finish():
            second()
            finish.done = True
            if then is not None:
                then()

        finish.done = False
        self.queue.append(first)
        self.release()
        self.held = finish
        return finish

    def vector(self, task, need=None):
        if need is not None and not need.done:
            if need is self.held:
                self.release()
            while not need.done:
                self.run(1)
        task()
        self.run(2)


class Copies:
    def __init__(self, sems):
        self.sems = sems
        self.count = 0

    def start(self, src, dst):
        copy = pltpu.make_async_copy(src, dst, self.sems.at[self.count])
        self.count += 1
        copy.start()
        return copy


def order_of(meta_ref, depth, slot):
    return jnp.bitwise_xor(jnp.bitwise_xor(slot, meta_ref[0]), meta_ref[1] * (depth - 1))


def shifts(meta_ref, p):
    return meta_ref[2 + 2 * p], meta_ref[3 + 2 * p]


def load_pieces(meta_ref, depth, copies, pieces, piece_refs, ext_ref, base, w):
    started = []
    for (slot, tile, plane), ref in zip(pieces, piece_refs):
        at = order_of(meta_ref, depth, slot) - base
        rows = pl.ds(tile * w, w)
        dst = ext_ref.at[at, :, rows, :] if plane is None else ext_ref.at[at, plane, rows, :]
        started.append(copies.start(ref, dst))
    return started


def times_window(meta_ref, ext_ref, at, p, wave_ref, write):
    w = wave_ref.shape[-1]
    r, q = (value.astype(jnp.int16) for value in shifts(meta_ref, p))
    cols = lax.broadcasted_iota(jnp.int16, (CHUNK, w), 1) < q
    index = lax.broadcasted_iota(jnp.int16, (CHUNK, w), 0)
    for start in range(0, w, CHUNK):
        rows = slice(start, start + CHUNK)
        below = slice(w + start, w + start + CHUNK)
        halo_row = index + jnp.int16(start) < r
        planes = []
        for plane in range(2):
            own = jnp.where(cols, ext_ref[at, plane, rows, w:], ext_ref[at, plane, rows, :w])
            halo = jnp.where(cols, ext_ref[at, plane, below, w:], ext_ref[at, plane, below, :w])
            planes.append(jnp.where(halo_row, halo, own).astype(f32))
        wr, wi = planes
        ar, ai = wave_ref[0, rows, :].astype(f32), wave_ref[1, rows, :].astype(f32)
        write(rows, ar * wr - ai * wi, ar * wi + ai * wr)


def to_product(x_ref):
    w = x_ref.shape[0]

    def write(rows, real, imag):
        x_ref[rows, :w] = real.astype(bf16)
        x_ref[rows, w:] = imag.astype(bf16)

    return write


def gradient_rows(meta_ref, g_ref, waves_a, waves_b, start):
    w = waves_a[0].shape[-1]
    rows = slice(start, start + CHUNK)
    index = lax.broadcasted_iota(jnp.int32, (CHUNK, w), 0) + start
    cols = lax.broadcasted_iota(jnp.int32, (CHUNK, w), 1)
    sums = [None, None]
    for p, (a_ref, b_ref) in enumerate(zip(waves_a, waves_b)):
        r, q = shifts(meta_ref, p)
        halo_row, right_col = index < r, cols < q
        ar, ai = a_ref[0, rows, :].astype(f32), a_ref[1, rows, :].astype(f32)
        br, bi = b_ref[0, rows, :].astype(f32), b_ref[1, rows, :].astype(f32)
        for plane, whole in enumerate((ar * br - ai * bi, -(ar * bi + ai * br))):
            halo = jnp.where(halo_row, whole, 0.0)
            parts = (
                whole,
                halo,
                jnp.where(right_col, whole, 0.0),
                jnp.where(right_col, halo, 0.0),
            )
            old = sums[plane]
            sums[plane] = parts if old is None else tuple(x + y for x, y in zip(old, parts))
    for plane in range(2):
        whole, halo, right, both = sums[plane]
        below = slice(w + start, w + start + CHUNK)
        g_ref[plane, rows, :w] = ((whole - halo) - (right - both)).astype(bf16)
        g_ref[plane, rows, w:] = (right - both).astype(bf16)
        g_ref[plane, below, :w] = (halo - both).astype(bf16)
        g_ref[plane, below, w:] = both.astype(bf16)


def gradient_parts(meta_ref, g_ref, waves_a, waves_b, parts):
    starts = list(range(0, waves_a[0].shape[-1], CHUNK))
    size = -(-len(starts) // parts)

    def task(part):
        def run():
            for start in starts[part * size : (part + 1) * size]:
                gradient_rows(meta_ref, g_ref, waves_a, waves_b, start)

        return run

    return [task(part) for part in range(parts)]


def each(ref, count):
    return [ref.at[i] for i in range(count)]


def start_kernel(
    probes, scale, meta_ref, probe_ref, cot_hbm, right_ref, left_ref, init_hbm, cot_ref, init_ref, x_ref, z_ref, sems
):
    w = probe_ref.shape[-1]
    copies = Copies(sems)
    high = meta_ref[1]
    kr, ki = float(scale.real), float(scale.imag)
    arriving = [
        copies.start(cot_hbm.at[meta_ref[0] * probes + p], cot_ref.at[p]) for p in range(probes)
    ]
    leaving = []
    tasks = Alternating()

    def moved(p, plane):
        r, q = shifts(meta_ref, p)
        return pltpu.roll(pltpu.roll(plane, r, 0), lax.rem(q, w), 1)

    def cotangent(p):
        arriving[p].wait()
        lr, li = moved(p, cot_ref[p, 0]), moved(p, cot_ref[p, 1])
        x_ref[p, :, :w] = (kr * lr + ki * li).astype(bf16)
        x_ref[p, :, w:] = (ki * lr - kr * li).astype(bf16)

    def spread(p):
        def leave():
            leaving.append(copies.start(init_ref.at[1, p], init_hbm.at[1 - high, p]))

        tasks.matrix(
            half_steps(x_ref.at[p], right_ref, left_ref, z_ref.at[p], [init_ref.at[1, p]]), leave
        )

    def launch(p):
        init_ref[0, p, 0] = moved(p, probe_ref[0]).astype(bf16)
        init_ref[0, p, 1] = moved(p, probe_ref[1]).astype(bf16)
        leaving.append(copies.start(init_ref.at[0, p], init_hbm.at[high, p]))

    for p in range(probes):
        tasks.vector(functools.partial(cotangent, p))
        spread(p)
        tasks.vector(functools.partial(launch, p))
    tasks.flush()
    for copy in leaving:
        copy.wait()


def near_kernel(probes, depth, pieces, meta_ref, _, right_ref, left_ref, *refs):
    n = len(pieces)
    half = depth // 2
    piece_refs, refs = refs[:n], refs[n:]
    waves_hbm, ext_ref, in_ref, a_ref, out_ref, x_ref, z_ref, sems = refs
    w = in_ref.shape[-1]
    copies = Copies(sems)
    arriving = [copies.start(waves_hbm.at[0, p], in_ref.at[p]) for p in range(probes)]
    for copy in load_pieces(meta_ref, depth, copies, pieces, piece_refs, ext_ref, 0, w):
        copy.wait()
    leaving = []
    tasks = Alternating()
    before = [None] * probes
    for k in range(half):
        for p in range(probes):
            if k == 0:
                arriving[p].wait()
            wave = in_ref.at[p] if k == 0 else a_ref.at[(k - 1) % 2, p]
            tasks.vector(
                lambda: times_window(meta_ref, ext_ref, k, p, wave, to_product(x_ref.at[p])),
                before[p],
            )
            outs = [out_ref.at[k, p]] + ([a_ref.at[k % 2, p]] if k < half - 1 else [])

            def leave(k=k, p=p):
                leaving.append(copies.start(out_ref.at[k, p], waves_hbm.at[2 + k, p]))

            before[p] = tasks.matrix(
                half_steps(x_ref.at[p], right_ref, left_ref, z_ref.at[p], outs), leave
            )
    tasks.flush()
    for copy in leaving:
        copy.wait()


def far_kernel(probes, depth, pieces, meta_ref, _, right_ref, left_ref, *refs):
    n = len(pieces)
    half = depth // 2
    piece_refs, refs = refs[:n], refs[n:]
    g_hbm, refs = refs[:half], refs[half:]
    waves_hbm, next_hbm, v_hbm, ext_ref, g_ref, in_ref, a_ref, b_ref, xa_ref, xb_ref, z_ref, sems = refs
    w = in_ref.shape[-1]
    high = meta_ref[1]
    copies = Copies(sems)
    a_in = [copies.start(waves_hbm.at[1 + half, p], in_ref.at[0, p]) for p in range(probes)]
    b_in = [copies.start(waves_hbm.at[1, p], in_ref.at[1, p]) for p in range(probes)]
    for copy in load_pieces(meta_ref, depth, copies, pieces, piece_refs, ext_ref, half, w):
        copy.wait()
    tasks = Alternating()
    a_waves = [each(in_ref.at[0], probes)]
    a_waves += [each(a_ref.at[k], probes) for k in range(half - 1)]
    before = [None] * probes
    for k in range(half - 1):
        for p in range(probes):
            if k == 0:
                a_in[p].wait()
            tasks.vector(
                lambda: times_window(
                    meta_ref, ext_ref, k, p, a_waves[k][p], to_product(xa_ref.at[p])
                ),
                before[p],
            )
            before[p] = tasks.matrix(
                half_steps(xa_ref.at[p], right_ref, left_ref, z_ref.at[p], [a_waves[k + 1][p]])
            )
    leaving = []
    before = [None] * probes
    for k in range(half):
        last = k == half - 1
        at = half - 1 - k
        b_now = each(in_ref.at[1] if k == 0 else b_ref.at[(k - 1) % 2], probes)
        for p in range(probes):
            if k == 0:
                b_in[p].wait()
            tasks.vector(
                lambda: times_window(meta_ref, ext_ref, at, p, b_now[p], to_product(xb_ref.at[p])),
                before[p],
            )
            if last:
                leaving.append(copies.start(xb_ref.at[p], next_hbm.at[p]))
        tasks.flush()
        parts = gradient_parts(meta_ref, g_ref.at[at], a_waves[at], b_now, probes)
        for p in range(probes):
            if not last:
                before[p] = tasks.matrix(
                    half_steps(
                        xb_ref.at[p], right_ref, left_ref, z_ref.at[p], [b_ref.at[k % 2, p]]
                    )
                )
        for p in range(probes):
            tasks.vector(parts[p])
        tasks.flush()
        if k == 0:

            @pl.when(high == 1)
            def _():
                for p in range(probes):

                    def write(rows, real, imag):
                        v_ref = xa_ref.at[p]
                        v_ref[rows, :w] = real.astype(bf16)
                        v_ref[rows, w:] = -imag.astype(bf16)

                    times_window(meta_ref, ext_ref, half - 1, p, a_waves[half - 1][p], write)

    leaving.append(copies.start(xa_ref, v_hbm))
    for slot in range(half):
        order = order_of(meta_ref, depth, slot + half) - half
        leaving.append(copies.start(g_ref.at[order], g_hbm[slot]))
    for copy in leaving:
        copy.wait()


def return_kernel(probes, depth, pieces, meta_ref, _, x_hbm, v_hbm, right_ref, left_ref, *refs):
    n = len(pieces)
    half = depth // 2
    piece_refs, refs = refs[:n], refs[n:]
    waves_hbm, lam_hbm, ext_ref, b_ref, out_ref, x_ref, v_ref, z_ref, t_ref, lam_ref, sems = refs
    w = x_ref.shape[1]
    copies = Copies(sems)
    x_in = [copies.start(x_hbm.at[p], x_ref.at[p]) for p in range(probes)]
    arrived = load_pieces(meta_ref, depth, copies, pieces, piece_refs, ext_ref, 0, w)
    arrived.append(copies.start(v_hbm, v_ref))
    tasks = Alternating()
    leaving = []

    def multiply(k, p):
        if k == 0 and p == 0:
            for copy in arrived:
                copy.wait()
        times_window(
            meta_ref, ext_ref, half - 1 - k, p, b_ref.at[k % 2, p], to_product(x_ref.at[p])
        )

    for k in range(half):
        ready = []
        for p in range(probes):
            if k == 0:
                x_in[p].wait()

            def leave(k=k, p=p):
                leaving.append(copies.start(out_ref.at[k, p], waves_hbm.at[2 + half + k, p]))

            outs = [b_ref.at[k % 2, p], out_ref.at[k, p]]
            ready.append(
                tasks.matrix(
                    half_steps(x_ref.at[p], right_ref, left_ref, z_ref.at[p], outs), leave
                )
            )
        for p in range(probes):
            tasks.vector(functools.partial(multiply, k, p), ready[p])
    tasks.flush()
    low = meta_ref[1] == 0
    for plane in range(2):
        total = None
        for p in range(probes):
            r, q = shifts(meta_ref, p)
            cols = slice(plane * w, (plane + 1) * w)
            mine = x_ref[p, :, cols].astype(f32)
            mine = -mine if plane else mine
            wave = jnp.where(low, mine, v_ref[p, :, cols].astype(f32))
            back = pltpu.roll(pltpu.roll(wave, lax.rem(w - r, w), 0), lax.rem(2 * w - q, w), 1)
            total = back if total is None else total + back
        t_ref[plane] = total
    rows = w // depth
    for slot in range(depth):
        block = pl.multiple_of(jnp.bitwise_xor(meta_ref[0], slot) * rows, rows)
        for plane in range(2):
            lam_ref[slot, plane] = t_ref[plane, pl.ds(block, rows), :].astype(bf16)
    leaving.append(copies.start(lam_ref, lam_hbm))
    for copy in leaving:
        copy.wait()


def gradient_kernel(probes, depth, meta_ref, _, *refs):
    half = depth // 2
    g_hbm, (waves_hbm, g_ref, a_ref, b_ref, sems) = refs[:half], refs[half:]
    copies = Copies(sems)
    arriving = []
    for k in range(half):
        order = half - 1 - k
        arriving.append(
            (
                copies.start(waves_hbm.at[1 + order if order else 0], a_ref.at[k]),
                copies.start(waves_hbm.at[2 + half + k], b_ref.at[k]),
            )
        )
    for k in range(half):
        for copy in arriving[k]:
            copy.wait()
        for part in gradient_parts(
            meta_ref,
            g_ref.at[half - 1 - k],
            each(a_ref.at[k], probes),
            each(b_ref.at[k], probes),
            1,
        ):
            part()
    leaving = [
        copies.start(g_ref.at[order_of(meta_ref, depth, slot)], g_hbm[slot]) for slot in range(half)
    ]
    for copy in leaving:
        copy.wait()


def cost(probes, steps, w):
    return pl.CostEstimate(
        flops=COST * probes * steps * 16 * w**3, bytes_accessed=8 * 2**20, transcendentals=0
    )

def after(value, *others):
    return lax.optimization_barrier((value, others))[0]


def total(first, second):
    return (first.astype(f32) + second.astype(f32)).astype(bf16)


def per_device(obj_slices, probe, positions, exit_cotangent):
    depth = lax.axis_size("depth")
    lat = lax.axis_size("lat")
    d = lax.axis_index("depth")
    w = probe.shape[-1]
    columns = obj_slices.shape[-1]
    half = depth // 2
    probes = positions.shape[0] // depth
    bits = [1 << i for i in range(depth.bit_length() - 1)]

    def across(value, bit):
        return lax.ppermute(value, "depth", [(i, i ^ bit) for i in range(depth)])

    def along(value, steps):
        return lax.ppermute(value, "lat", [(i, (i + steps) % lat) for i in range(lat)])

    def along_xor(value, bit):
        return lax.ppermute(value, "lat", [(i, i ^ bit) for i in range(lat)])

    right, left = sides(w)
    right, left = jnp.asarray(right), jnp.asarray(left)
    scale = gain ** (-2 * depth)
    own = obj_slices[0].astype(bf16)

    my_positions = lax.dynamic_slice(positions, (d * probes, 0), (probes, 2))
    meta = jnp.concatenate(
        [jnp.stack([d, (d >= half).astype(jnp.int32)]).astype(jnp.int32), my_positions.reshape(-1)]
    )

    smem = pl.BlockSpec(memory_space=pltpu.SMEM)
    vmem = pl.BlockSpec(memory_space=pltpu.VMEM)
    anywhere = pl.BlockSpec(memory_space=pl.ANY)
    hbm = pl.BlockSpec(memory_space=pltpu.HBM)
    wave = (probes, 2, w, w)
    product = (probes, w, 2 * w)
    g_shape = (2, 2 * w, columns)
    z_scratch = pltpu.VMEM((probes, 2 * w, w), bf16)
    ext_scratch = pltpu.VMEM((half, 2, 2 * w, columns), bf16)

    def call(kernel, name, steps, outs, ins, scratch, copies, limit=VMEM_LIMIT, aliases={}):
        flat, structure = jax.tree.flatten(outs)
        results = pl.pallas_call(
            kernel,
            out_shape=flat,
            in_specs=[spec for spec, _ in ins],
            out_specs=[anywhere] * len(flat),
            scratch_shapes=scratch + [pltpu.SemaphoreType.DMA((copies,))],
            compiler_params=pltpu.CompilerParams(vmem_limit_bytes=limit),
            cost_estimate=cost(probes, steps, w),
            input_output_aliases=aliases,
            name=name,
        )(*[array for _, array in ins])
        return jax.tree.unflatten(structure, results)

    shape = jax.ShapeDtypeStruct
    sides_in = [(vmem, right), (vmem, left)]

    rows = max(2 + depth, 32 * 2**20 // (4 * probes * w * w))
    all_waves = shape((rows,) + wave, bf16)
    init = call(
        functools.partial(start_kernel, probes, scale),
        "first_waves",
        1,
        all_waves,
        [(smem, meta), (vmem, probe), (hbm, exit_cotangent)] + sides_in,
        [
            pltpu.VMEM(wave, f32),
            pltpu.VMEM((2,) + wave, bf16),
            pltpu.VMEM(product, bf16),
            z_scratch,
        ],
        3 * probes,
        60 * 2**20,
    )

    tiles = {0: own}
    halos = {0: along(own, -1)}
    for bit in reversed(bits[1:]):
        for slot in sorted(tiles):
            tiles[slot | bit] = across(tiles[slot], bit)
        for slot in sorted(s for s in tiles if s & bit):
            kept = halos[slot ^ bit]
            kept = kept if isinstance(kept, tuple) else (kept[0], kept[1])
            halos[slot] = (
                across(after(kept[0], init), bit),
                along(after(tiles[slot][1], init), -1),
            )

    def to_both_cores(slots, earlier):
        for slot in slots:
            sent = tiles[slot] if slot == 0 else after(tiles[slot], earlier)
            tiles[slot | 1] = across(sent, 1)
            halos[slot | 1] = jax.tree.map(lambda x: across(after(x, earlier), 1), halos[slot])

    def pieces_of(slots):
        names, arrays = [], []
        for slot in slots:
            names.append((slot, 0, None))
            arrays.append((anywhere, tiles[slot]))
            if isinstance(halos[slot], tuple):
                for plane in range(2):
                    names.append((slot, 1, plane))
                    arrays.append((anywhere, halos[slot][plane]))
            else:
                names.append((slot, 1, None))
                arrays.append((anywhere, halos[slot]))
        return names, arrays

    to_both_cores(range(0, half, 2), init)
    names, arrays = pieces_of(range(half))
    waves = call(
        functools.partial(near_kernel, probes, depth, names),
        "near_slices",
        half,
        all_waves,
        [(smem, meta), (hbm, init)] + sides_in + arrays,
        [
            ext_scratch,
            pltpu.VMEM(wave, bf16),
            pltpu.VMEM((2,) + wave, f32),
            pltpu.VMEM((half,) + wave, bf16),
            pltpu.VMEM(product, bf16),
            z_scratch,
        ],
        probes * (half + 1) + len(names),
        aliases={1: 0},
    )

    to_both_cores(range(half, depth, 2), waves)
    far_names, far_arrays = pieces_of(range(half, depth))
    far_grads, waves, next_x, v = call(
        functools.partial(far_kernel, probes, depth, far_names),
        "far_slices",
        half,
        ([shape(g_shape, bf16)] * half, all_waves, shape(product, bf16), shape(product, bf16)),
        [(smem, meta), (hbm, waves)] + sides_in + far_arrays,
        [
            ext_scratch,
            pltpu.VMEM((half,) + g_shape, bf16),
            pltpu.VMEM((2,) + wave, bf16),
            pltpu.VMEM((half - 1,) + wave, f32),
            pltpu.VMEM((2,) + wave, f32),
            pltpu.VMEM(product, bf16),
            pltpu.VMEM(product, bf16),
            z_scratch,
        ],
        3 * probes + len(far_names) + half + 1,
        aliases={1: half},
    )

    waves, part = call(
        functools.partial(return_kernel, probes, depth, names),
        "return_waves",
        half,
        (all_waves, shape((depth, 2, w // depth, w), bf16)),
        [(smem, meta), (hbm, waves), (hbm, next_x), (hbm, v)] + sides_in + arrays,
        [
            ext_scratch,
            pltpu.VMEM((2,) + wave, f32),
            pltpu.VMEM((half,) + wave, bf16),
            pltpu.VMEM(product, bf16),
            pltpu.VMEM(product, bf16),
            z_scratch,
            pltpu.VMEM((2, w, w), f32),
            pltpu.VMEM((depth, 2, w // depth, w), bf16),
        ],
        probes * (half + 1) + len(names) + 2,
        aliases={1: 0},
    )

    def core_sums(grads):
        return {
            slot: total(grads[slot], across(grads[slot | 1], 1)) for slot in grads if not slot & 1
        }

    far_sums = core_sums({slot + half: g for slot, g in enumerate(far_grads)})
    owns, halo_grads = {}, {}
    for slot, both in far_sums.items():
        both = after(both, waves)
        owns[slot] = (both[0, :w], both[1, :w])
        halo_grads[slot] = (both[0, w:], both[1, w:])
    shifted = {slot: along(halo_grads[slot][1], 1) for slot in owns}
    crossed = {slot: across(halo_grads[slot][0], half) for slot in owns if slot & half}
    part_sum = part[0].astype(f32)
    arriving = [across(part[slot], slot) for slot in range(1, depth)]
    near_grads, _ = call(
        functools.partial(gradient_kernel, probes, depth),
        "near_gradients",
        half,
        ([shape(g_shape, bf16)] * half, all_waves),
        [(smem, after(meta, far_sums)), (hbm, waves)],
        [
            pltpu.VMEM((half,) + g_shape, bf16),
            pltpu.VMEM((half,) + wave, bf16),
            pltpu.VMEM((half,) + wave, bf16),
        ],
        3 * half,
        aliases={1: half},
    )
    for moved in after(arriving, near_grads):
        part_sum = part_sum + moved.astype(f32)
    part = part_sum.astype(bf16)
    shifted, crossed = after((shifted, crossed), near_grads)
    for slot in list(owns):
        real, imag = owns[slot]
        owns[slot] = (real, total(imag, shifted[slot]))
    near_grads = after(near_grads, owns, crossed, part)
    near_sums = core_sums(dict(enumerate(near_grads)))
    lat_bits = [1 << i for i in range(lat.bit_length() - 1)]
    butterfly = not lat & (lat - 1)
    if butterfly:
        moved = along_xor(part, lat_bits[0])
        part = total(part, after(moved, near_sums))
    for slot, both in near_sums.items():
        halo_grads[slot] = (both[0, w:], both[1, w:])
        both = after(both, halo_grads[slot], part)
        owns[slot] = (both[0, :w], both[1, :w])
    from_below = None
    for bit in bits[1:]:
        for slot in sorted((s for s in owns if s & bit), reverse=True):
            halo_real, halo_imag = halo_grads.pop(slot)
            real, imag = owns.pop(slot)
            halo_real = crossed[slot] if bit == half else across(halo_real, bit)
            if slot not in shifted:
                imag = total(imag, along(halo_imag, 1))
            sent = across(jnp.stack([real, imag]), bit)
            kept = halo_grads[slot ^ bit]
            halo_grads[slot ^ bit] = (total(kept[0], halo_real), kept[1])
            if len(halo_grads) == 1:
                from_below = along(jnp.stack(halo_grads[0]), 1)
                sent = after(sent, from_below)
            kept = owns[slot ^ bit]
            owns[slot ^ bit] = (total(kept[0], sent[0]), total(kept[1], sent[1]))
    object_grad = (jnp.stack(owns[0]).astype(f32) + from_below.astype(f32))[None]

    if butterfly:
        for bit in lat_bits[1:]:
            part = total(part, along_xor(part, bit))
    else:
        part = lax.psum(part.astype(f32), "lat")
    return (object_grad, part.astype(f32))


def solution(mesh):
    placed = (P("depth", None, "lat", None), P(), P("lat", None), P("lat", None, None, None))
    return jax.shard_map(
        per_device,
        mesh=mesh,
        in_specs=placed,
        out_specs=(P("depth", None, "lat", None), P(None, "depth", None)),
        check_vma=False,
    )
```

```python
import functools
import math

import jax
import jax.numpy as jnp
import ml_dtypes
import numpy as np
from jax import lax
from jax.experimental import pallas as pl
from jax.experimental.pallas import tpu as pltpu
from jax.sharding import PartitionSpec as P

defocus_scale = 0.7
gain = 1.457627118644068 * np.exp(0.14208207981059368j)
f32 = jnp.float32
bf16 = jnp.bfloat16
CHUNK = 16
VMEM_LIMIT = 36 * 2**20
COST = 6


def propagator(size):
    index = np.arange(size)
    signed = np.where(index < size // 2, index, index - size).astype(np.float64)
    chirp = -math.pi * defocus_scale * signed * signed / size
    angles = 2.0 * math.pi * ((index[:, None] * index[None, :]) % size) / size + chirp[None, :]
    kernel = np.exp(1j * angles).sum(axis=1) / size
    return kernel[(index[:, None] - index[None, :]) % size] * gain


def sides(size):
    matrix = propagator(size)
    real, imag = matrix.real, matrix.imag
    right = np.block([[real, imag], [-imag, real]])
    left = np.block([[real, -imag], [imag, real]])
    return right.astype(ml_dtypes.bfloat16), left.astype(ml_dtypes.bfloat16)


def half_steps(x_ref, right_ref, left_ref, z_ref, out_refs):
    w = z_ref.shape[1]

    def first():
        z = jnp.dot(x_ref[...], right_ref[...], preferred_element_type=f32)
        z_ref[:w] = z[:, :w].astype(bf16)
        z_ref[w:] = z[:, w:].astype(bf16)

    def second():
        y = jnp.dot(left_ref[...], z_ref[...], preferred_element_type=f32)
        for out_ref in out_refs:
            out_ref[0] = y[:w].astype(out_ref.dtype)
            out_ref[1] = y[w:].astype(out_ref.dtype)

    return first, second


class Alternating:
    def __init__(self):
        self.queue = []
        self.held = None

    def release(self):
        if self.held is not None:
            self.queue.append(self.held)
        self.held = None

    def run(self, count):
        for task in self.queue[:count]:
            task()
        del self.queue[:count]

    def flush(self):
        self.release()
        self.run(len(self.queue))

    def matrix(self, steps, then=None):
        first, second = steps

        def finish():
            second()
            finish.done = True
            if then is not None:
                then()

        finish.done = False
        self.queue.append(first)
        self.release()
        self.held = finish
        return finish

    def vector(self, task, need=None):
        if need is not None and not need.done:
            if need is self.held:
                self.release()
            while not need.done:
                self.run(1)
        task()
        self.run(2)


class Copies:
    def __init__(self, sems):
        self.sems = sems
        self.count = 0

    def start(self, src, dst):
        copy = pltpu.make_async_copy(src, dst, self.sems.at[self.count])
        self.count += 1
        copy.start()
        return copy


def order_of(meta_ref, depth, slot):
    return jnp.bitwise_xor(jnp.bitwise_xor(slot, meta_ref[0]), meta_ref[1] * (depth - 1))


def shifts(meta_ref, p):
    return meta_ref[2 + 2 * p], meta_ref[3 + 2 * p]


def load_pieces(meta_ref, depth, copies, pieces, piece_refs, ext_ref, base, w):
    started = []
    for (slot, tile, plane), ref in zip(pieces, piece_refs):
        at = order_of(meta_ref, depth, slot) - base
        rows = pl.ds(tile * w, w)
        dst = ext_ref.at[at, :, rows, :] if plane is None else ext_ref.at[at, plane, rows, :]
        started.append(copies.start(ref, dst))
    return started


def times_window(meta_ref, ext_ref, at, p, wave_ref, write):
    w = wave_ref.shape[-1]
    r, q = (value.astype(jnp.int16) for value in shifts(meta_ref, p))
    cols = lax.broadcasted_iota(jnp.int16, (CHUNK, w), 1) < q
    index = lax.broadcasted_iota(jnp.int16, (CHUNK, w), 0)
    for start in range(0, w, CHUNK):
        rows = slice(start, start + CHUNK)
        below = slice(w + start, w + start + CHUNK)
        halo_row = index + jnp.int16(start) < r
        planes = []
        for plane in range(2):
            own = jnp.where(cols, ext_ref[at, plane, rows, w:], ext_ref[at, plane, rows, :w])
            halo = jnp.where(cols, ext_ref[at, plane, below, w:], ext_ref[at, plane, below, :w])
            planes.append(jnp.where(halo_row, halo, own).astype(f32))
        wr, wi = planes
        ar, ai = wave_ref[0, rows, :].astype(f32), wave_ref[1, rows, :].astype(f32)
        write(rows, ar * wr - ai * wi, ar * wi + ai * wr)


def to_product(x_ref):
    w = x_ref.shape[0]

    def write(rows, real, imag):
        x_ref[rows, :w] = real.astype(bf16)
        x_ref[rows, w:] = imag.astype(bf16)

    return write


def gradient_rows(meta_ref, g_ref, waves_a, waves_b, start):
    w = waves_a[0].shape[-1]
    rows = slice(start, start + CHUNK)
    index = lax.broadcasted_iota(jnp.int32, (CHUNK, w), 0) + start
    cols = lax.broadcasted_iota(jnp.int32, (CHUNK, w), 1)
    sums = [None, None]
    for p, (a_ref, b_ref) in enumerate(zip(waves_a, waves_b)):
        r, q = shifts(meta_ref, p)
        halo_row, right_col = index < r, cols < q
        ar, ai = a_ref[0, rows, :].astype(f32), a_ref[1, rows, :].astype(f32)
        br, bi = b_ref[0, rows, :].astype(f32), b_ref[1, rows, :].astype(f32)
        for plane, whole in enumerate((ar * br - ai * bi, -(ar * bi + ai * br))):
            halo = jnp.where(halo_row, whole, 0.0)
            parts = (
                whole,
                halo,
                jnp.where(right_col, whole, 0.0),
                jnp.where(right_col, halo, 0.0),
            )
            old = sums[plane]
            sums[plane] = parts if old is None else tuple(x + y for x, y in zip(old, parts))
    for plane in range(2):
        whole, halo, right, both = sums[plane]
        below = slice(w + start, w + start + CHUNK)
        g_ref[plane, rows, :w] = ((whole - halo) - (right - both)).astype(bf16)
        g_ref[plane, rows, w:] = (right - both).astype(bf16)
        g_ref[plane, below, :w] = (halo - both).astype(bf16)
        g_ref[plane, below, w:] = both.astype(bf16)


def gradient_parts(meta_ref, g_ref, waves_a, waves_b, parts):
    starts = list(range(0, waves_a[0].shape[-1], CHUNK))
    size = -(-len(starts) // parts)

    def task(part):
        def run():
            for start in starts[part * size : (part + 1) * size]:
                gradient_rows(meta_ref, g_ref, waves_a, waves_b, start)

        return run

    return [task(part) for part in range(parts)]


def each(ref, count):
    return [ref.at[i] for i in range(count)]


def start_kernel(
    probes, scale, meta_ref, probe_ref, cot_hbm, right_ref, left_ref, init_hbm, cot_ref, init_ref, x_ref, z_ref, sems
):
    w = probe_ref.shape[-1]
    copies = Copies(sems)
    high = meta_ref[1]
    kr, ki = float(scale.real), float(scale.imag)
    arriving = [
        copies.start(cot_hbm.at[meta_ref[0] * probes + p], cot_ref.at[p]) for p in range(probes)
    ]
    leaving = []
    tasks = Alternating()

    def moved(p, plane):
        r, q = shifts(meta_ref, p)
        return pltpu.roll(pltpu.roll(plane, r, 0), lax.rem(q, w), 1)

    def cotangent(p):
        arriving[p].wait()
        lr, li = moved(p, cot_ref[p, 0]), moved(p, cot_ref[p, 1])
        x_ref[p, :, :w] = (kr * lr + ki * li).astype(bf16)
        x_ref[p, :, w:] = (ki * lr - kr * li).astype(bf16)

    def spread(p):
        def leave():
            leaving.append(copies.start(init_ref.at[1, p], init_hbm.at[1 - high, p]))

        tasks.matrix(
            half_steps(x_ref.at[p], right_ref, left_ref, z_ref.at[p], [init_ref.at[1, p]]), leave
        )

    def launch(p):
        init_ref[0, p, 0] = moved(p, probe_ref[0]).astype(bf16)
        init_ref[0, p, 1] = moved(p, probe_ref[1]).astype(bf16)
        leaving.append(copies.start(init_ref.at[0, p], init_hbm.at[high, p]))

    for p in range(probes):
        tasks.vector(functools.partial(cotangent, p))
        spread(p)
        tasks.vector(functools.partial(launch, p))
    tasks.flush()
    for copy in leaving:
        copy.wait()


def near_kernel(probes, depth, pieces, meta_ref, _, right_ref, left_ref, *refs):
    n = len(pieces)
    half = depth // 2
    piece_refs, refs = refs[:n], refs[n:]
    waves_hbm, ext_ref, in_ref, a_ref, out_ref, x_ref, z_ref, sems = refs
    w = in_ref.shape[-1]
    copies = Copies(sems)
    arriving = [copies.start(waves_hbm.at[0, p], in_ref.at[p]) for p in range(probes)]
    for copy in load_pieces(meta_ref, depth, copies, pieces, piece_refs, ext_ref, 0, w):
        copy.wait()
    leaving = []
    tasks = Alternating()
    before = [None] * probes
    for k in range(half):
        for p in range(probes):
            if k == 0:
                arriving[p].wait()
            wave = in_ref.at[p] if k == 0 else a_ref.at[(k - 1) % 2, p]
            tasks.vector(
                lambda: times_window(meta_ref, ext_ref, k, p, wave, to_product(x_ref.at[p])),
                before[p],
            )
            outs = [out_ref.at[k, p]] + ([a_ref.at[k % 2, p]] if k < half - 1 else [])

            def leave(k=k, p=p):
                leaving.append(copies.start(out_ref.at[k, p], waves_hbm.at[2 + k, p]))

            before[p] = tasks.matrix(
                half_steps(x_ref.at[p], right_ref, left_ref, z_ref.at[p], outs), leave
            )
    tasks.flush()
    for copy in leaving:
        copy.wait()


def far_kernel(probes, depth, pieces, meta_ref, _, right_ref, left_ref, *refs):
    n = len(pieces)
    half = depth // 2
    piece_refs, refs = refs[:n], refs[n:]
    g_hbm, refs = refs[:half], refs[half:]
    waves_hbm, next_hbm, v_hbm, ext_ref, g_ref, in_ref, a_ref, b_ref, xa_ref, xb_ref, z_ref, sems = refs
    w = in_ref.shape[-1]
    high = meta_ref[1]
    copies = Copies(sems)
    a_in = [copies.start(waves_hbm.at[1 + half, p], in_ref.at[0, p]) for p in range(probes)]
    b_in = [copies.start(waves_hbm.at[1, p], in_ref.at[1, p]) for p in range(probes)]
    for copy in load_pieces(meta_ref, depth, copies, pieces, piece_refs, ext_ref, half, w):
        copy.wait()
    tasks = Alternating()
    a_waves = [each(in_ref.at[0], probes)]
    a_waves += [each(a_ref.at[k], probes) for k in range(half - 1)]
    before = [None] * probes
    for k in range(half - 1):
        for p in range(probes):
            if k == 0:
                a_in[p].wait()
            tasks.vector(
                lambda: times_window(
                    meta_ref, ext_ref, k, p, a_waves[k][p], to_product(xa_ref.at[p])
                ),
                before[p],
            )
            before[p] = tasks.matrix(
                half_steps(xa_ref.at[p], right_ref, left_ref, z_ref.at[p], [a_waves[k + 1][p]])
            )
    leaving = []
    before = [None] * probes
    for k in range(half):
        last = k == half - 1
        at = half - 1 - k
        b_now = each(in_ref.at[1] if k == 0 else b_ref.at[(k - 1) % 2], probes)
        for p in range(probes):
            if k == 0:
                b_in[p].wait()
            tasks.vector(
                lambda: times_window(meta_ref, ext_ref, at, p, b_now[p], to_product(xb_ref.at[p])),
                before[p],
            )
            if last:
                leaving.append(copies.start(xb_ref.at[p], next_hbm.at[p]))
        tasks.flush()
        parts = gradient_parts(meta_ref, g_ref.at[at], a_waves[at], b_now, probes)
        for p in range(probes):
            if not last:
                before[p] = tasks.matrix(
                    half_steps(
                        xb_ref.at[p], right_ref, left_ref, z_ref.at[p], [b_ref.at[k % 2, p]]
                    )
                )
        for p in range(probes):
            tasks.vector(parts[p])
        tasks.flush()
        if k == 0:

            @pl.when(high == 1)
            def _():
                for p in range(probes):

                    def write(rows, real, imag):
                        v_ref = xa_ref.at[p]
                        v_ref[rows, :w] = real.astype(bf16)
                        v_ref[rows, w:] = -imag.astype(bf16)

                    times_window(meta_ref, ext_ref, half - 1, p, a_waves[half - 1][p], write)

    leaving.append(copies.start(xa_ref, v_hbm))
    for slot in range(half):
        order = order_of(meta_ref, depth, slot + half) - half
        leaving.append(copies.start(g_ref.at[order], g_hbm[slot]))
    for copy in leaving:
        copy.wait()


def return_kernel(probes, depth, pieces, meta_ref, _, x_hbm, v_hbm, right_ref, left_ref, *refs):
    n = len(pieces)
    half = depth // 2
    piece_refs, refs = refs[:n], refs[n:]
    waves_hbm, lam_hbm, ext_ref, b_ref, out_ref, x_ref, v_ref, z_ref, t_ref, lam_ref, sems = refs
    w = x_ref.shape[1]
    copies = Copies(sems)
    x_in = [copies.start(x_hbm.at[p], x_ref.at[p]) for p in range(probes)]
    arrived = load_pieces(meta_ref, depth, copies, pieces, piece_refs, ext_ref, 0, w)
    arrived.append(copies.start(v_hbm, v_ref))
    tasks = Alternating()
    leaving = []

    def multiply(k, p):
        if k == 0 and p == 0:
            for copy in arrived:
                copy.wait()
        times_window(
            meta_ref, ext_ref, half - 1 - k, p, b_ref.at[k % 2, p], to_product(x_ref.at[p])
        )

    for k in range(half):
        ready = []
        for p in range(probes):
            if k == 0:
                x_in[p].wait()

            def leave(k=k, p=p):
                leaving.append(copies.start(out_ref.at[k, p], waves_hbm.at[2 + half + k, p]))

            outs = [b_ref.at[k % 2, p], out_ref.at[k, p]]
            ready.append(
                tasks.matrix(
                    half_steps(x_ref.at[p], right_ref, left_ref, z_ref.at[p], outs), leave
                )
            )
        for p in range(probes):
            tasks.vector(functools.partial(multiply, k, p), ready[p])
    tasks.flush()
    low = meta_ref[1] == 0
    for plane in range(2):
        total = None
        for p in range(probes):
            r, q = shifts(meta_ref, p)
            cols = slice(plane * w, (plane + 1) * w)
            mine = x_ref[p, :, cols].astype(f32)
            mine = -mine if plane else mine
            wave = jnp.where(low, mine, v_ref[p, :, cols].astype(f32))
            back = pltpu.roll(pltpu.roll(wave, lax.rem(w - r, w), 0), lax.rem(2 * w - q, w), 1)
            total = back if total is None else total + back
        t_ref[plane] = total
    rows = w // depth
    for slot in range(depth):
        block = pl.multiple_of(jnp.bitwise_xor(meta_ref[0], slot) * rows, rows)
        for plane in range(2):
            lam_ref[slot, plane] = t_ref[plane, pl.ds(block, rows), :].astype(bf16)
    leaving.append(copies.start(lam_ref, lam_hbm))
    for copy in leaving:
        copy.wait()


def gradient_kernel(probes, depth, meta_ref, _, *refs):
    half = depth // 2
    g_hbm, (waves_hbm, g_ref, a_ref, b_ref, sems) = refs[:half], refs[half:]
    copies = Copies(sems)
    arriving = []
    for k in range(half):
        order = half - 1 - k
        arriving.append(
            (
                copies.start(waves_hbm.at[1 + order if order else 0], a_ref.at[k]),
                copies.start(waves_hbm.at[2 + half + k], b_ref.at[k]),
            )
        )
    for k in range(half):
        for copy in arriving[k]:
            copy.wait()
        for part in gradient_parts(
            meta_ref,
            g_ref.at[half - 1 - k],
            each(a_ref.at[k], probes),
            each(b_ref.at[k], probes),
            1,
        ):
            part()
    leaving = [
        copies.start(g_ref.at[order_of(meta_ref, depth, slot)], g_hbm[slot]) for slot in range(half)
    ]
    for copy in leaving:
        copy.wait()


def cost(probes, steps, w):
    return pl.CostEstimate(
        flops=COST * probes * steps * 16 * w**3, bytes_accessed=8 * 2**20, transcendentals=0
    )

def after(value, *others):
    return lax.optimization_barrier((value, others))[0]


def total(first, second):
    return (first.astype(f32) + second.astype(f32)).astype(bf16)


def per_device(obj_slices, probe, positions, exit_cotangent):
    depth = lax.axis_size("depth")
    lat = lax.axis_size("lat")
    d = lax.axis_index("depth")
    w = probe.shape[-1]
    columns = obj_slices.shape[-1]
    half = depth // 2
    probes = positions.shape[0] // depth
    bits = [1 << i for i in range(depth.bit_length() - 1)]

    def across(value, bit):
        return lax.ppermute(value, "depth", [(i, i ^ bit) for i in range(depth)])

    def along(value, steps):
        return lax.ppermute(value, "lat", [(i, (i + steps) % lat) for i in range(lat)])

    def along_xor(value, bit):
        return lax.ppermute(value, "lat", [(i, i ^ bit) for i in range(lat)])

    right, left = sides(w)
    right, left = jnp.asarray(right), jnp.asarray(left)
    scale = gain ** (-2 * depth)
    own = obj_slices[0].astype(bf16)

    my_positions = lax.dynamic_slice(positions, (d * probes, 0), (probes, 2))
    meta = jnp.concatenate(
        [jnp.stack([d, (d >= half).astype(jnp.int32)]).astype(jnp.int32), my_positions.reshape(-1)]
    )

    smem = pl.BlockSpec(memory_space=pltpu.SMEM)
    vmem = pl.BlockSpec(memory_space=pltpu.VMEM)
    anywhere = pl.BlockSpec(memory_space=pl.ANY)
    hbm = pl.BlockSpec(memory_space=pltpu.HBM)
    wave = (probes, 2, w, w)
    product = (probes, w, 2 * w)
    g_shape = (2, 2 * w, columns)
    z_scratch = pltpu.VMEM((probes, 2 * w, w), bf16)
    ext_scratch = pltpu.VMEM((half, 2, 2 * w, columns), bf16)

    def call(kernel, name, steps, outs, ins, scratch, copies, limit=VMEM_LIMIT, aliases={}):
        flat, structure = jax.tree.flatten(outs)
        results = pl.pallas_call(
            kernel,
            out_shape=flat,
            in_specs=[spec for spec, _ in ins],
            out_specs=[anywhere] * len(flat),
            scratch_shapes=scratch + [pltpu.SemaphoreType.DMA((copies,))],
            compiler_params=pltpu.CompilerParams(vmem_limit_bytes=limit),
            cost_estimate=cost(probes, steps, w),
            input_output_aliases=aliases,
            name=name,
        )(*[array for _, array in ins])
        return jax.tree.unflatten(structure, results)

    shape = jax.ShapeDtypeStruct
    sides_in = [(vmem, right), (vmem, left)]

    rows = max(2 + depth, 32 * 2**20 // (4 * probes * w * w))
    all_waves = shape((rows,) + wave, bf16)
    init = call(
        functools.partial(start_kernel, probes, scale),
        "first_waves",
        1,
        all_waves,
        [(smem, meta), (vmem, probe), (hbm, exit_cotangent)] + sides_in,
        [
            pltpu.VMEM(wave, f32),
            pltpu.VMEM((2,) + wave, bf16),
            pltpu.VMEM(product, bf16),
            z_scratch,
        ],
        3 * probes,
        60 * 2**20,
    )

    tiles = {0: own}
    halos = {0: along(own, -1)}
    for bit in reversed(bits[1:]):
        for slot in sorted(tiles):
            tiles[slot | bit] = across(tiles[slot], bit)
        for slot in sorted(s for s in tiles if s & bit):
            kept = halos[slot ^ bit]
            kept = kept if isinstance(kept, tuple) else (kept[0], kept[1])
            halos[slot] = (
                across(after(kept[0], init), bit),
                along(after(tiles[slot][1], init), -1),
            )

    def to_both_cores(slots, earlier):
        for slot in slots:
            sent = tiles[slot] if slot == 0 else after(tiles[slot], earlier)
            tiles[slot | 1] = across(sent, 1)
            halos[slot | 1] = jax.tree.map(lambda x: across(after(x, earlier), 1), halos[slot])

    def pieces_of(slots):
        names, arrays = [], []
        for slot in slots:
            names.append((slot, 0, None))
            arrays.append((anywhere, tiles[slot]))
            if isinstance(halos[slot], tuple):
                for plane in range(2):
                    names.append((slot, 1, plane))
                    arrays.append((anywhere, halos[slot][plane]))
            else:
                names.append((slot, 1, None))
                arrays.append((anywhere, halos[slot]))
        return names, arrays

    to_both_cores(range(0, half, 2), init)
    names, arrays = pieces_of(range(half))
    waves = call(
        functools.partial(near_kernel, probes, depth, names),
        "near_slices",
        half,
        all_waves,
        [(smem, meta), (hbm, init)] + sides_in + arrays,
        [
            ext_scratch,
            pltpu.VMEM(wave, bf16),
            pltpu.VMEM((2,) + wave, f32),
            pltpu.VMEM((half,) + wave, bf16),
            pltpu.VMEM(product, bf16),
            z_scratch,
        ],
        probes * (half + 1) + len(names),
        aliases={1: 0},
    )

    to_both_cores(range(half, depth, 2), waves)
    far_names, far_arrays = pieces_of(range(half, depth))
    far_grads, waves, next_x, v = call(
        functools.partial(far_kernel, probes, depth, far_names),
        "far_slices",
        half,
        ([shape(g_shape, bf16)] * half, all_waves, shape(product, bf16), shape(product, bf16)),
        [(smem, meta), (hbm, waves)] + sides_in + far_arrays,
        [
            ext_scratch,
            pltpu.VMEM((half,) + g_shape, bf16),
            pltpu.VMEM((2,) + wave, bf16),
            pltpu.VMEM((half - 1,) + wave, f32),
            pltpu.VMEM((2,) + wave, f32),
            pltpu.VMEM(product, bf16),
            pltpu.VMEM(product, bf16),
            z_scratch,
        ],
        3 * probes + len(far_names) + half + 1,
        aliases={1: half},
    )

    waves, part = call(
        functools.partial(return_kernel, probes, depth, names),
        "return_waves",
        half,
        (all_waves, shape((depth, 2, w // depth, w), bf16)),
        [(smem, meta), (hbm, waves), (hbm, next_x), (hbm, v)] + sides_in + arrays,
        [
            ext_scratch,
            pltpu.VMEM((2,) + wave, f32),
            pltpu.VMEM((half,) + wave, bf16),
            pltpu.VMEM(product, bf16),
            pltpu.VMEM(product, bf16),
            z_scratch,
            pltpu.VMEM((2, w, w), f32),
            pltpu.VMEM((depth, 2, w // depth, w), bf16),
        ],
        probes * (half + 1) + len(names) + 2,
        aliases={1: 0},
    )

    def core_sums(grads):
        return {
            slot: total(grads[slot], across(grads[slot | 1], 1)) for slot in grads if not slot & 1
        }

    far_sums = core_sums({slot + half: g for slot, g in enumerate(far_grads)})
    owns, halo_grads = {}, {}
    for slot, both in far_sums.items():
        both = after(both, waves)
        owns[slot] = (both[0, :w], both[1, :w])
        halo_grads[slot] = (both[0, w:], both[1, w:])
    shifted = {slot: along(halo_grads[slot][1], 1) for slot in owns}
    crossed = {slot: across(halo_grads[slot][0], half) for slot in owns if slot & half}
    part_sum = part[0].astype(f32)
    arriving = [across(part[slot], slot) for slot in range(1, depth)]
    near_grads, _ = call(
        functools.partial(gradient_kernel, probes, depth),
        "near_gradients",
        half,
        ([shape(g_shape, bf16)] * half, all_waves),
        [(smem, after(meta, far_sums)), (hbm, waves)],
        [
            pltpu.VMEM((half,) + g_shape, bf16),
            pltpu.VMEM((half,) + wave, bf16),
            pltpu.VMEM((half,) + wave, bf16),
        ],
        3 * half,
        aliases={1: half},
    )
    for moved in after(arriving, near_grads):
        part_sum = part_sum + moved.astype(f32)
    part = part_sum.astype(bf16)
    shifted, crossed = after((shifted, crossed), near_grads)
    for slot in list(owns):
        real, imag = owns[slot]
        owns[slot] = (real, total(imag, shifted[slot]))
    near_grads = after(near_grads, owns, crossed, part)
    near_sums = core_sums(dict(enumerate(near_grads)))
    power_of_two = not lat & (lat - 1)
    if power_of_two:
        part_sum = part.astype(f32)
        arriving = {other: along_xor(part, other) for other in range(1, lat // 2)}
        near_sums, arriving = after((near_sums, arriving))
        for moved in arriving.values():
            part_sum = part_sum + moved.astype(f32)
        part = part_sum.astype(bf16)
    for slot, both in near_sums.items():
        halo_grads[slot] = (both[0, w:], both[1, w:])
        both = after(both, halo_grads[slot], part)
        owns[slot] = (both[0, :w], both[1, :w])
    from_below = None
    for bit in bits[1:]:
        for slot in sorted((s for s in owns if s & bit), reverse=True):
            halo_real, halo_imag = halo_grads.pop(slot)
            real, imag = owns.pop(slot)
            halo_real = crossed[slot] if bit == half else across(halo_real, bit)
            if slot not in shifted:
                imag = total(imag, along(halo_imag, 1))
            sent = across(jnp.stack([real, imag]), bit)
            kept = halo_grads[slot ^ bit]
            halo_grads[slot ^ bit] = (total(kept[0], halo_real), kept[1])
            if len(halo_grads) == 1:
                from_below = along(jnp.stack(halo_grads[0]), 1)
                sent = after(sent, from_below)
            kept = owns[slot ^ bit]
            owns[slot ^ bit] = (total(kept[0], sent[0]), total(kept[1], sent[1]))
    object_grad = (jnp.stack(owns[0]).astype(f32) + from_below.astype(f32))[None]

    if power_of_two:
        part = total(part, along_xor(part, lat // 2))
    else:
        part = lax.psum(part.astype(f32), "lat")
    return (object_grad, part.astype(f32))


def solution(mesh):
    placed = (P("depth", None, "lat", None), P(), P("lat", None), P("lat", None, None, None))
    return jax.shard_map(
        per_device,
        mesh=mesh,
        in_specs=placed,
        out_specs=(P("depth", None, "lat", None), P(None, "depth", None)),
        check_vma=False,
    )
```

```python
import functools
import math

import jax
import jax.numpy as jnp
import ml_dtypes
import numpy as np
from jax import lax
from jax.experimental import pallas as pl
from jax.experimental.pallas import tpu as pltpu
from jax.sharding import PartitionSpec as P

defocus_scale = 0.7
gain = 1.457627118644068 * np.exp(0.14208207981059368j)
f32 = jnp.float32
bf16 = jnp.bfloat16
CHUNK = 16
VMEM_LIMIT = 36 * 2**20
COST = 6


def propagator(size):
    index = np.arange(size)
    signed = np.where(index < size // 2, index, index - size).astype(np.float64)
    chirp = -math.pi * defocus_scale * signed * signed / size
    angles = 2.0 * math.pi * ((index[:, None] * index[None, :]) % size) / size + chirp[None, :]
    kernel = np.exp(1j * angles).sum(axis=1) / size
    return kernel[(index[:, None] - index[None, :]) % size] * gain


def sides(size):
    matrix = propagator(size)
    real, imag = matrix.real, matrix.imag
    right = np.block([[real, imag], [-imag, real]])
    left = np.block([[real, -imag], [imag, real]])
    return right.astype(ml_dtypes.bfloat16), left.astype(ml_dtypes.bfloat16)


def half_steps(x_ref, right_ref, left_ref, z_ref, out_refs):
    w = z_ref.shape[1]

    def first():
        z = jnp.dot(x_ref[...], right_ref[...], preferred_element_type=f32)
        z_ref[:w] = z[:, :w].astype(bf16)
        z_ref[w:] = z[:, w:].astype(bf16)

    def second():
        y = jnp.dot(left_ref[...], z_ref[...], preferred_element_type=f32)
        for out_ref in out_refs:
            out_ref[0] = y[:w].astype(out_ref.dtype)
            out_ref[1] = y[w:].astype(out_ref.dtype)

    return first, second


class Alternating:
    def __init__(self):
        self.queue = []
        self.held = None

    def release(self):
        if self.held is not None:
            self.queue.append(self.held)
        self.held = None

    def run(self, count):
        for task in self.queue[:count]:
            task()
        del self.queue[:count]

    def flush(self):
        self.release()
        self.run(len(self.queue))

    def matrix(self, steps, then=None):
        first, second = steps

        def finish():
            second()
            finish.done = True
            if then is not None:
                then()

        finish.done = False
        self.queue.append(first)
        self.release()
        self.held = finish
        return finish

    def vector(self, task, need=None):
        if need is not None and not need.done:
            if need is self.held:
                self.release()
            while not need.done:
                self.run(1)
        task()
        self.run(2)


class Copies:
    def __init__(self, sems):
        self.sems = sems
        self.count = 0

    def start(self, src, dst):
        copy = pltpu.make_async_copy(src, dst, self.sems.at[self.count])
        self.count += 1
        copy.start()
        return copy


def order_of(meta_ref, depth, slot):
    return jnp.bitwise_xor(jnp.bitwise_xor(slot, meta_ref[0]), meta_ref[1] * (depth - 1))


def shifts(meta_ref, p):
    return meta_ref[2 + 2 * p], meta_ref[3 + 2 * p]


def load_pieces(meta_ref, depth, copies, pieces, piece_refs, ext_ref, base, w):
    started = []
    for (slot, tile, plane), ref in zip(pieces, piece_refs):
        at = order_of(meta_ref, depth, slot) - base
        rows = pl.ds(tile * w, w)
        dst = ext_ref.at[at, :, rows, :] if plane is None else ext_ref.at[at, plane, rows, :]
        started.append(copies.start(ref, dst))
    return started


def times_window(meta_ref, ext_ref, at, p, wave_ref, write):
    w = wave_ref.shape[-1]
    r, q = (value.astype(jnp.int16) for value in shifts(meta_ref, p))
    cols = lax.broadcasted_iota(jnp.int16, (CHUNK, w), 1) < q
    index = lax.broadcasted_iota(jnp.int16, (CHUNK, w), 0)
    for start in range(0, w, CHUNK):
        rows = slice(start, start + CHUNK)
        below = slice(w + start, w + start + CHUNK)
        halo_row = index + jnp.int16(start) < r
        planes = []
        for plane in range(2):
            own = jnp.where(cols, ext_ref[at, plane, rows, w:], ext_ref[at, plane, rows, :w])
            halo = jnp.where(cols, ext_ref[at, plane, below, w:], ext_ref[at, plane, below, :w])
            planes.append(jnp.where(halo_row, halo, own).astype(f32))
        wr, wi = planes
        ar, ai = wave_ref[0, rows, :].astype(f32), wave_ref[1, rows, :].astype(f32)
        write(rows, ar * wr - ai * wi, ar * wi + ai * wr)


def to_product(x_ref):
    w = x_ref.shape[0]

    def write(rows, real, imag):
        x_ref[rows, :w] = real.astype(bf16)
        x_ref[rows, w:] = imag.astype(bf16)

    return write


def gradient_rows(meta_ref, g_ref, waves_a, waves_b, start):
    w = waves_a[0].shape[-1]
    rows = slice(start, start + CHUNK)
    index = lax.broadcasted_iota(jnp.int32, (CHUNK, w), 0) + start
    cols = lax.broadcasted_iota(jnp.int32, (CHUNK, w), 1)
    sums = [None, None]
    for p, (a_ref, b_ref) in enumerate(zip(waves_a, waves_b)):
        r, q = shifts(meta_ref, p)
        halo_row, right_col = index < r, cols < q
        ar, ai = a_ref[0, rows, :].astype(f32), a_ref[1, rows, :].astype(f32)
        br, bi = b_ref[0, rows, :].astype(f32), b_ref[1, rows, :].astype(f32)
        for plane, whole in enumerate((ar * br - ai * bi, -(ar * bi + ai * br))):
            halo = jnp.where(halo_row, whole, 0.0)
            parts = (
                whole,
                halo,
                jnp.where(right_col, whole, 0.0),
                jnp.where(right_col, halo, 0.0),
            )
            old = sums[plane]
            sums[plane] = parts if old is None else tuple(x + y for x, y in zip(old, parts))
    for plane in range(2):
        whole, halo, right, both = sums[plane]
        below = slice(w + start, w + start + CHUNK)
        g_ref[plane, rows, :w] = ((whole - halo) - (right - both)).astype(bf16)
        g_ref[plane, rows, w:] = (right - both).astype(bf16)
        g_ref[plane, below, :w] = (halo - both).astype(bf16)
        g_ref[plane, below, w:] = both.astype(bf16)


def gradient_parts(meta_ref, g_ref, waves_a, waves_b, parts):
    starts = list(range(0, waves_a[0].shape[-1], CHUNK))
    size = -(-len(starts) // parts)

    def task(part):
        def run():
            for start in starts[part * size : (part + 1) * size]:
                gradient_rows(meta_ref, g_ref, waves_a, waves_b, start)

        return run

    return [task(part) for part in range(parts)]


def each(ref, count):
    return [ref.at[i] for i in range(count)]


def start_kernel(
    probes, scale, meta_ref, probe_ref, cot_hbm, right_ref, left_ref, init_hbm, cot_ref, init_ref, x_ref, z_ref, sems
):
    w = probe_ref.shape[-1]
    copies = Copies(sems)
    high = meta_ref[1]
    kr, ki = float(scale.real), float(scale.imag)
    arriving = [
        copies.start(cot_hbm.at[meta_ref[0] * probes + p], cot_ref.at[p]) for p in range(probes)
    ]
    leaving = []
    tasks = Alternating()

    def moved(p, plane):
        r, q = shifts(meta_ref, p)
        return pltpu.roll(pltpu.roll(plane, r, 0), lax.rem(q, w), 1)

    def cotangent(p):
        arriving[p].wait()
        lr, li = moved(p, cot_ref[p, 0]), moved(p, cot_ref[p, 1])
        x_ref[p, :, :w] = (kr * lr + ki * li).astype(bf16)
        x_ref[p, :, w:] = (ki * lr - kr * li).astype(bf16)

    def spread(p):
        def leave():
            leaving.append(copies.start(init_ref.at[1, p], init_hbm.at[1 - high, p]))

        tasks.matrix(
            half_steps(x_ref.at[p], right_ref, left_ref, z_ref.at[p], [init_ref.at[1, p]]), leave
        )

    def launch(p):
        init_ref[0, p, 0] = moved(p, probe_ref[0]).astype(bf16)
        init_ref[0, p, 1] = moved(p, probe_ref[1]).astype(bf16)
        leaving.append(copies.start(init_ref.at[0, p], init_hbm.at[high, p]))

    for p in range(probes):
        tasks.vector(functools.partial(cotangent, p))
        spread(p)
        tasks.vector(functools.partial(launch, p))
    tasks.flush()
    for copy in leaving:
        copy.wait()


def near_kernel(probes, depth, pieces, meta_ref, _, right_ref, left_ref, *refs):
    n = len(pieces)
    half = depth // 2
    piece_refs, refs = refs[:n], refs[n:]
    waves_hbm, ext_ref, in_ref, a_ref, out_ref, x_ref, z_ref, sems = refs
    w = in_ref.shape[-1]
    copies = Copies(sems)
    arriving = [copies.start(waves_hbm.at[0, p], in_ref.at[p]) for p in range(probes)]
    for copy in load_pieces(meta_ref, depth, copies, pieces, piece_refs, ext_ref, 0, w):
        copy.wait()
    leaving = []
    tasks = Alternating()
    before = [None] * probes
    for k in range(half):
        for p in range(probes):
            if k == 0:
                arriving[p].wait()
            wave = in_ref.at[p] if k == 0 else a_ref.at[(k - 1) % 2, p]
            tasks.vector(
                lambda: times_window(meta_ref, ext_ref, k, p, wave, to_product(x_ref.at[p])),
                before[p],
            )
            outs = [out_ref.at[k, p]] + ([a_ref.at[k % 2, p]] if k < half - 1 else [])

            def leave(k=k, p=p):
                leaving.append(copies.start(out_ref.at[k, p], waves_hbm.at[2 + k, p]))

            before[p] = tasks.matrix(
                half_steps(x_ref.at[p], right_ref, left_ref, z_ref.at[p], outs), leave
            )
    tasks.flush()
    for copy in leaving:
        copy.wait()


def far_kernel(probes, depth, pieces, meta_ref, _, right_ref, left_ref, *refs):
    n = len(pieces)
    half = depth // 2
    piece_refs, refs = refs[:n], refs[n:]
    g_hbm, refs = refs[:half], refs[half:]
    waves_hbm, next_hbm, v_hbm, ext_ref, g_ref, in_ref, a_ref, b_ref, xa_ref, xb_ref, z_ref, sems = refs
    w = in_ref.shape[-1]
    high = meta_ref[1]
    copies = Copies(sems)
    a_in = [copies.start(waves_hbm.at[1 + half, p], in_ref.at[0, p]) for p in range(probes)]
    b_in = [copies.start(waves_hbm.at[1, p], in_ref.at[1, p]) for p in range(probes)]
    for copy in load_pieces(meta_ref, depth, copies, pieces, piece_refs, ext_ref, half, w):
        copy.wait()
    tasks = Alternating()
    a_waves = [each(in_ref.at[0], probes)]
    a_waves += [each(a_ref.at[k], probes) for k in range(half - 1)]
    before = [None] * probes
    for k in range(half - 1):
        for p in range(probes):
            if k == 0:
                a_in[p].wait()
            tasks.vector(
                lambda: times_window(
                    meta_ref, ext_ref, k, p, a_waves[k][p], to_product(xa_ref.at[p])
                ),
                before[p],
            )
            before[p] = tasks.matrix(
                half_steps(xa_ref.at[p], right_ref, left_ref, z_ref.at[p], [a_waves[k + 1][p]])
            )
    leaving = []
    before = [None] * probes
    for k in range(half):
        last = k == half - 1
        at = half - 1 - k
        b_now = each(in_ref.at[1] if k == 0 else b_ref.at[(k - 1) % 2], probes)
        for p in range(probes):
            if k == 0:
                b_in[p].wait()
            tasks.vector(
                lambda: times_window(meta_ref, ext_ref, at, p, b_now[p], to_product(xb_ref.at[p])),
                before[p],
            )
            if last:
                leaving.append(copies.start(xb_ref.at[p], next_hbm.at[p]))
        tasks.flush()
        parts = gradient_parts(meta_ref, g_ref.at[at], a_waves[at], b_now, probes)
        for p in range(probes):
            if not last:
                before[p] = tasks.matrix(
                    half_steps(
                        xb_ref.at[p], right_ref, left_ref, z_ref.at[p], [b_ref.at[k % 2, p]]
                    )
                )
        for p in range(probes):
            tasks.vector(parts[p])
        tasks.flush()
        if k == 0:

            @pl.when(high == 1)
            def _():
                for p in range(probes):

                    def write(rows, real, imag):
                        v_ref = xa_ref.at[p]
                        v_ref[rows, :w] = real.astype(bf16)
                        v_ref[rows, w:] = -imag.astype(bf16)

                    times_window(meta_ref, ext_ref, half - 1, p, a_waves[half - 1][p], write)

    leaving.append(copies.start(xa_ref, v_hbm))
    for slot in range(half):
        order = order_of(meta_ref, depth, slot + half) - half
        leaving.append(copies.start(g_ref.at[order], g_hbm[slot]))
    for copy in leaving:
        copy.wait()


def return_kernel(probes, depth, pieces, meta_ref, _, x_hbm, v_hbm, right_ref, left_ref, *refs):
    n = len(pieces)
    half = depth // 2
    piece_refs, refs = refs[:n], refs[n:]
    waves_hbm, lam_hbm, ext_ref, b_ref, out_ref, x_ref, v_ref, z_ref, t_ref, lam_ref, sems = refs
    w = x_ref.shape[1]
    copies = Copies(sems)
    x_in = [copies.start(x_hbm.at[p], x_ref.at[p]) for p in range(probes)]
    arrived = load_pieces(meta_ref, depth, copies, pieces, piece_refs, ext_ref, 0, w)
    arrived.append(copies.start(v_hbm, v_ref))
    tasks = Alternating()
    leaving = []

    def multiply(k, p):
        if k == 0 and p == 0:
            for copy in arrived:
                copy.wait()
        times_window(
            meta_ref, ext_ref, half - 1 - k, p, b_ref.at[k % 2, p], to_product(x_ref.at[p])
        )

    for k in range(half):
        ready = []
        for p in range(probes):
            if k == 0:
                x_in[p].wait()

            def leave(k=k, p=p):
                leaving.append(copies.start(out_ref.at[k, p], waves_hbm.at[2 + half + k, p]))

            outs = [b_ref.at[k % 2, p], out_ref.at[k, p]]
            ready.append(
                tasks.matrix(
                    half_steps(x_ref.at[p], right_ref, left_ref, z_ref.at[p], outs), leave
                )
            )
        for p in range(probes):
            tasks.vector(functools.partial(multiply, k, p), ready[p])
    tasks.flush()
    low = meta_ref[1] == 0
    for plane in range(2):
        total = None
        for p in range(probes):
            r, q = shifts(meta_ref, p)
            cols = slice(plane * w, (plane + 1) * w)
            mine = x_ref[p, :, cols].astype(f32)
            mine = -mine if plane else mine
            wave = jnp.where(low, mine, v_ref[p, :, cols].astype(f32))
            back = pltpu.roll(pltpu.roll(wave, lax.rem(w - r, w), 0), lax.rem(2 * w - q, w), 1)
            total = back if total is None else total + back
        t_ref[plane] = total
    rows = w // depth
    for slot in range(depth):
        block = pl.multiple_of(jnp.bitwise_xor(meta_ref[0], slot) * rows, rows)
        for plane in range(2):
            lam_ref[slot, plane] = t_ref[plane, pl.ds(block, rows), :].astype(bf16)
    leaving.append(copies.start(lam_ref, lam_hbm))
    for copy in leaving:
        copy.wait()


def gradient_kernel(probes, depth, meta_ref, _, *refs):
    half = depth // 2
    g_hbm, (waves_hbm, g_ref, a_ref, b_ref, sems) = refs[:half], refs[half:]
    copies = Copies(sems)
    arriving = []
    for k in range(half):
        order = half - 1 - k
        arriving.append(
            (
                copies.start(waves_hbm.at[1 + order if order else 0], a_ref.at[k]),
                copies.start(waves_hbm.at[2 + half + k], b_ref.at[k]),
            )
        )
    for k in range(half):
        for copy in arriving[k]:
            copy.wait()
        for part in gradient_parts(
            meta_ref,
            g_ref.at[half - 1 - k],
            each(a_ref.at[k], probes),
            each(b_ref.at[k], probes),
            1,
        ):
            part()
    leaving = [
        copies.start(g_ref.at[order_of(meta_ref, depth, slot)], g_hbm[slot]) for slot in range(half)
    ]
    for copy in leaving:
        copy.wait()


def cost(probes, steps, w):
    return pl.CostEstimate(
        flops=COST * probes * steps * 16 * w**3, bytes_accessed=8 * 2**20, transcendentals=0
    )

def after(value, *others):
    return lax.optimization_barrier((value, others))[0]


def total(first, second):
    return (first.astype(f32) + second.astype(f32)).astype(bf16)


def per_device(obj_slices, probe, positions, exit_cotangent):
    depth = lax.axis_size("depth")
    lat = lax.axis_size("lat")
    d = lax.axis_index("depth")
    w = probe.shape[-1]
    columns = obj_slices.shape[-1]
    half = depth // 2
    probes = positions.shape[0] // depth
    bits = [1 << i for i in range(depth.bit_length() - 1)]

    def across(value, bit):
        return lax.ppermute(value, "depth", [(i, i ^ bit) for i in range(depth)])

    def along(value, steps):
        return lax.ppermute(value, "lat", [(i, (i + steps) % lat) for i in range(lat)])

    def along_xor(value, bit):
        return lax.ppermute(value, "lat", [(i, i ^ bit) for i in range(lat)])

    right, left = sides(w)
    right, left = jnp.asarray(right), jnp.asarray(left)
    scale = gain ** (-2 * depth)
    own = obj_slices[0].astype(bf16)

    my_positions = lax.dynamic_slice(positions, (d * probes, 0), (probes, 2))
    meta = jnp.concatenate(
        [jnp.stack([d, (d >= half).astype(jnp.int32)]).astype(jnp.int32), my_positions.reshape(-1)]
    )

    smem = pl.BlockSpec(memory_space=pltpu.SMEM)
    vmem = pl.BlockSpec(memory_space=pltpu.VMEM)
    anywhere = pl.BlockSpec(memory_space=pl.ANY)
    hbm = pl.BlockSpec(memory_space=pltpu.HBM)
    wave = (probes, 2, w, w)
    product = (probes, w, 2 * w)
    g_shape = (2, 2 * w, columns)
    z_scratch = pltpu.VMEM((probes, 2 * w, w), bf16)
    ext_scratch = pltpu.VMEM((half, 2, 2 * w, columns), bf16)

    def call(kernel, name, steps, outs, ins, scratch, copies, limit=VMEM_LIMIT, aliases={}):
        flat, structure = jax.tree.flatten(outs)
        results = pl.pallas_call(
            kernel,
            out_shape=flat,
            in_specs=[spec for spec, _ in ins],
            out_specs=[anywhere] * len(flat),
            scratch_shapes=scratch + [pltpu.SemaphoreType.DMA((copies,))],
            compiler_params=pltpu.CompilerParams(vmem_limit_bytes=limit),
            cost_estimate=cost(probes, steps, w),
            input_output_aliases=aliases,
            name=name,
        )(*[array for _, array in ins])
        return jax.tree.unflatten(structure, results)

    shape = jax.ShapeDtypeStruct
    sides_in = [(vmem, right), (vmem, left)]

    rows = max(2 + depth, 32 * 2**20 // (4 * probes * w * w))
    all_waves = shape((rows,) + wave, bf16)
    init = call(
        functools.partial(start_kernel, probes, scale),
        "first_waves",
        1,
        all_waves,
        [(smem, meta), (vmem, probe), (hbm, exit_cotangent)] + sides_in,
        [
            pltpu.VMEM(wave, f32),
            pltpu.VMEM((2,) + wave, bf16),
            pltpu.VMEM(product, bf16),
            z_scratch,
        ],
        3 * probes,
        60 * 2**20,
    )

    tiles = {0: own}
    halos = {0: along(own, -1)}
    for bit in reversed(bits[1:]):
        for slot in sorted(tiles):
            tiles[slot | bit] = across(tiles[slot], bit)
        for slot in sorted(s for s in tiles if s & bit):
            kept = halos[slot ^ bit]
            kept = kept if isinstance(kept, tuple) else (kept[0], kept[1])
            halos[slot] = (
                across(after(kept[0], init), bit),
                along(after(tiles[slot][1], init), -1),
            )

    def to_both_cores(slots, earlier):
        for slot in slots:
            sent = tiles[slot] if slot == 0 else after(tiles[slot], earlier)
            tiles[slot | 1] = across(sent, 1)
            halos[slot | 1] = jax.tree.map(lambda x: across(after(x, earlier), 1), halos[slot])

    def pieces_of(slots):
        names, arrays = [], []
        for slot in slots:
            names.append((slot, 0, None))
            arrays.append((anywhere, tiles[slot]))
            if isinstance(halos[slot], tuple):
                for plane in range(2):
                    names.append((slot, 1, plane))
                    arrays.append((anywhere, halos[slot][plane]))
            else:
                names.append((slot, 1, None))
                arrays.append((anywhere, halos[slot]))
        return names, arrays

    to_both_cores(range(0, half, 2), init)
    names, arrays = pieces_of(range(half))
    waves = call(
        functools.partial(near_kernel, probes, depth, names),
        "near_slices",
        half,
        all_waves,
        [(smem, meta), (hbm, init)] + sides_in + arrays,
        [
            ext_scratch,
            pltpu.VMEM(wave, bf16),
            pltpu.VMEM((2,) + wave, f32),
            pltpu.VMEM((half,) + wave, bf16),
            pltpu.VMEM(product, bf16),
            z_scratch,
        ],
        probes * (half + 1) + len(names),
        aliases={1: 0},
    )

    to_both_cores(range(half, depth, 2), waves)
    far_names, far_arrays = pieces_of(range(half, depth))
    far_grads, waves, next_x, v = call(
        functools.partial(far_kernel, probes, depth, far_names),
        "far_slices",
        half,
        ([shape(g_shape, bf16)] * half, all_waves, shape(product, bf16), shape(product, bf16)),
        [(smem, meta), (hbm, waves)] + sides_in + far_arrays,
        [
            ext_scratch,
            pltpu.VMEM((half,) + g_shape, bf16),
            pltpu.VMEM((2,) + wave, bf16),
            pltpu.VMEM((half - 1,) + wave, f32),
            pltpu.VMEM((2,) + wave, f32),
            pltpu.VMEM(product, bf16),
            pltpu.VMEM(product, bf16),
            z_scratch,
        ],
        3 * probes + len(far_names) + half + 1,
        aliases={1: half},
    )

    waves, part = call(
        functools.partial(return_kernel, probes, depth, names),
        "return_waves",
        half,
        (all_waves, shape((depth, 2, w // depth, w), bf16)),
        [(smem, meta), (hbm, waves), (hbm, next_x), (hbm, v)] + sides_in + arrays,
        [
            ext_scratch,
            pltpu.VMEM((2,) + wave, f32),
            pltpu.VMEM((half,) + wave, bf16),
            pltpu.VMEM(product, bf16),
            pltpu.VMEM(product, bf16),
            z_scratch,
            pltpu.VMEM((2, w, w), f32),
            pltpu.VMEM((depth, 2, w // depth, w), bf16),
        ],
        probes * (half + 1) + len(names) + 2,
        aliases={1: 0},
    )

    def core_sums(grads):
        return {
            slot: total(grads[slot], across(grads[slot | 1], 1)) for slot in grads if not slot & 1
        }

    far_sums = core_sums({slot + half: g for slot, g in enumerate(far_grads)})
    owns, halo_grads = {}, {}
    for slot, both in far_sums.items():
        both = after(both, waves)
        owns[slot] = (both[0, :w], both[1, :w])
        halo_grads[slot] = (both[0, w:], both[1, w:])
    shifted = {slot: along(halo_grads[slot][1], 1) for slot in owns}
    crossed = {slot: across(halo_grads[slot][0], half) for slot in owns if half == 2}
    part_sum = part[0].astype(f32)
    arriving = [across(part[slot], slot) for slot in range(1, depth)]
    near_grads, _ = call(
        functools.partial(gradient_kernel, probes, depth),
        "near_gradients",
        half,
        ([shape(g_shape, bf16)] * half, all_waves),
        [(smem, after(meta, far_sums)), (hbm, waves)],
        [
            pltpu.VMEM((half,) + g_shape, bf16),
            pltpu.VMEM((half,) + wave, bf16),
            pltpu.VMEM((half,) + wave, bf16),
        ],
        3 * half,
        aliases={1: half},
    )
    for moved in after(arriving, near_grads):
        part_sum = part_sum + moved.astype(f32)
    part = part_sum.astype(bf16)
    near_sums = core_sums(dict(enumerate(near_grads)))
    lat_bits = [1 << i for i in range(lat.bit_length() - 1)]
    butterfly = not lat & (lat - 1)
    if butterfly:
        moved = along_xor(part, lat_bits[0])
        part = total(part, after(moved, near_sums))
    for slot, both in near_sums.items():
        halo_grads[slot] = (both[0, w:], both[1, w:])
        both = after(both, halo_grads[slot], part)
        owns[slot] = (both[0, :w], both[1, :w])
    from_below = None
    for bit in bits[1:]:
        for slot in sorted((s for s in owns if s & bit), reverse=True):
            halo_real, halo_imag = halo_grads.pop(slot)
            real, imag = owns.pop(slot)
            halo_real = crossed[slot] if slot in crossed else across(halo_real, bit)
            kept = halo_grads[slot ^ bit]
            halo_grads[slot ^ bit] = (total(kept[0], halo_real), kept[1])
            moved = shifted[slot] if slot in shifted else along(halo_imag, 1)
            if len(halo_grads) == 1:
                stacked = jnp.stack(halo_grads[0])
                from_below = along(stacked, 1)
                moved = after(moved, stacked)
            sent = across(jnp.stack([real, total(imag, moved)]), bit)
            if from_below is not None:
                sent = after(sent, from_below)
            kept = owns[slot ^ bit]
            owns[slot ^ bit] = (total(kept[0], sent[0]), total(kept[1], sent[1]))
    object_grad = (jnp.stack(owns[0]).astype(f32) + from_below.astype(f32))[None]

    if butterfly:
        for bit in lat_bits[1:]:
            part = total(part, along_xor(part, bit))
    else:
        part = lax.psum(part.astype(f32), "lat")
    return (object_grad, part.astype(f32))


def solution(mesh):
    placed = (P("depth", None, "lat", None), P(), P("lat", None), P("lat", None, None, None))
    return jax.shard_map(
        per_device,
        mesh=mesh,
        in_specs=placed,
        out_specs=(P("depth", None, "lat", None), P(None, "depth", None)),
        check_vma=False,
    )
```
